256 devices in a mesh: section: 4 (over y), sample: 32 (over z, x), replica: 2 (over core).
Axes of the slice: x: 4, y: 4, z: 8, core: 2. Of those that a mesh axis runs over, the one named last changes fastest.
Arguments:
- saved_input: bfloat16 [4, 2, 64, 128, 512], P('section', None, ('sample', 'replica')), may hold values from -6 to 6
- out_grad: bfloat16 [2, 64, 128, 512], P(None, ('sample', 'replica')), may hold values from -4 to 4
- w_in: bfloat16 [4, 512, 2048], P('section'), may hold values from -0.25 to 0.25
- w_out: bfloat16 [4, 512, 512], P('section'), may hold values from -0.25 to 0.25
- item_owner: int32 [64, 2, 128, 1], P(('sample', 'replica')), may hold values from 0 to 127; in each aligned block of 64 rows (0 to 63, 64 to 127, ..., all dimensions but the last counted through in order) at most 2 rows name the same one
- item_slot: int32 [64, 2, 128], P(('sample', 'replica')), may hold values from 0 to 511
- table: float32 [65536, 512], P(('section', 'sample')), may hold values from -4 to 4
- moment: float32 [65536, 512], P(('section', 'sample')), may hold values from -3 to 3
- second: float32 [65536], P(('section', 'sample')), may hold values from 0.01 to 1
Outputs:
- grad_in: float32 [4, 512, 2048], P('section', 'sample')
- grad_out: float32 [4, 512, 512], P('section', 'sample')
- table_new: float32 [65536, 512], P(('section', 'sample'))
- moment_new: float32 [65536, 512], P(('section', 'sample'))
- second_new: float32 [65536], P(('section', 'sample'))
The draws below stay inside these ranges and needn't reach their ends.
Inputs may be any that keep to these rules, and one draw needn't show every extreme that they name: `item_owner`: in each aligned block of 64 tokens, in the order sequence, micro-batch, position, no owner is named by more than 2 tokens.
All inputs are finite; a program needn't handle non-finite values.
Results may differ from the reference program's by a relative error of at most 0.029.
Values may be sent and summed in bfloat16 or wider, within the bound.
A program may use at most 128 MiB of HBM per device.

```python
import math
import jax
import jax.numpy as jnp
import numpy as np
from jax import lax

D = 512
HEADS = 4
SEQ_LEN = 128
MICRO = 2
LAYERS = 4
BLOCK = 64
ROWS_OWN = 512
OWNERS = 128
ROW_CAP = 2
ROWS = 65536
SEQS = 64
TOKENS = 16384


def touch_ends(result, key, low, largest):
    spot = [jax.random.randint(jax.random.fold_in(key, axis), (), 0, length) for axis, length in enumerate(result.shape)]
    widest = result.shape.index(max(result.shape))
    beside = spot[:widest] + [(spot[widest] + 1) % result.shape[widest]] + spot[widest + 1:]
    return result.at[tuple(spot)].set(low).at[tuple(beside)].set(largest)


def block_scale(key, dims, cuts, smallest, top_value):
    factor_of = 1.0
    for axis_at, shards_of in cuts:
        heights = jax.random.uniform(jax.random.fold_in(jax.random.fold_in(key, 6), axis_at), (shards_of,), jnp.float32, smallest / len(cuts), top_value / len(cuts))
        factor_of = factor_of * jnp.repeat(jnp.exp(heights), dims[axis_at] // shards_of).reshape((-1,) + (1,) * (len(dims) - 1 - axis_at))
    return factor_of


def rank_bounds(amount, lean):
    loads = [(1 << 20) // math.isqrt(standing ** lean) + 1 for standing in range(1, amount + 1)]
    scale = 1 + sum(loads) // (1 << 30)
    return np.cumsum(np.array([max(1, weight // scale) for weight in loads]))


def ranked(key, dims, count, skew):
    grid = rank_bounds(count, skew)
    pick = jax.random.randint(jax.random.fold_in(key, 1), dims, 0, int(grid[count - 1]))
    standing = jnp.searchsorted(jnp.asarray(grid, jnp.int32), pick, side="right")
    return jax.random.permutation(jax.random.fold_in(key, 2), count)[standing].astype(jnp.int32)


def routed_block(key, own, number, rows, number_of, top, limit, lean):
    sequence = jax.random.permutation(key, number_of)
    crowded, usual = shares(number_of, rows * top, limit, lean, True), shares(number_of, rows * top, limit, lean, False)
    places = jnp.arange(number_of)

    def named(sizes, turn):
        used = int((sizes > 0).sum())
        fixed = max(1, used // 4)
        shifted = fixed + (places - fixed + turn * (used - fixed)) % max(1, number_of - fixed)
        return jnp.zeros((number_of,), jnp.int32).at[sequence[jnp.where(places < fixed, places, shifted)]].set(jnp.asarray(sizes, jnp.int32))

    sizes = jnp.where(number % 4 == 0, named(crowded, number // 4), named(usual, number - number // 4 - 1))
    mixed = jax.random.permutation(jax.random.fold_in(own, 3), number_of)
    source_of, sink = mixed[0:number_of // 2 * 2:2], mixed[1:number_of // 2 * 2:2]
    margin = jnp.minimum(sizes[source_of] - 1, limit - sizes[sink]) // 2
    margin = jnp.where((source_of == sequence[0]) | (sink == sequence[0]) | (sizes[sink] == 0), 0, jnp.maximum(margin, 0))
    shifted = jax.random.randint(jax.random.fold_in(own, 4), (number_of // 2,), 0, 1 << 20) % (margin + 1)
    sizes = sizes.at[source_of].add(-shifted).at[sink].add(shifted)
    members = jnp.searchsorted(jnp.cumsum(sizes), jnp.arange(rows * top), side="right").astype(jnp.int32)
    table = members.reshape(top, rows).T
    table = table[jax.random.permutation(jax.random.fold_in(own, 1), rows)]
    turn = jax.random.randint(jax.random.fold_in(own, 2), (rows, 1), 0, top)
    return jnp.take_along_axis(table, (jnp.arange(top)[None, :] + turn) % top, axis=1)


def shares(amount, total, most, skew, full):
    loads = [(1 << 20) // math.isqrt(standing ** skew) + 1 for standing in range(1, amount + 1)]
    largest = most if full else min(most, max(-(-total // amount), total * loads[0] // sum(loads)))
    least = 1 if total - largest >= amount - 1 else 0
    given, spare = [largest] + [least] * (amount - 1), total - largest - least * (amount - 1)
    while spare > 0:
        movable = [i for i in range(1, amount) if given[i] < largest] or [i for i in range(1, amount) if given[i] < most]
        whole, budget = sum([loads[i] for i in movable]), spare
        for i in movable:
            addition = min(most - given[i], max(1, budget * loads[i] // whole), spare)
            given[i] = given[i] + addition
            spare = spare - addition
    return np.array(given)


def normal_values(rng, extent, scale, reach, pieces=(), dtype=jnp.bfloat16):
    result = scale * jax.random.normal(rng, extent, jnp.float32)
    if pieces:
        result = result * block_scale(rng, extent, pieces, -0.22, 0.18)
    return jnp.clip(result, -reach, reach).astype(dtype)


def setup_inputs(seed: int = 0) -> dict:
    arg_keys = jax.random.split(jax.random.key(seed), 10)
    saved_input = normal_values(arg_keys[0], (LAYERS, MICRO, SEQS, SEQ_LEN, D), 1.0, 6.0, ((0, 4), (2, 64)))
    out_grad = normal_values(arg_keys[1], (MICRO, SEQS, SEQ_LEN, D), 0.5, 4.0, ((1, 64),))
    w_in = normal_values(arg_keys[2], (LAYERS, D, 4 * D), D ** -0.5, 0.25, ((0, 4),))
    w_out = normal_values(arg_keys[3], (LAYERS, D, D), D ** -0.5, 0.25, ((0, 4),))
    item_owner_keys = jax.random.split(jax.random.fold_in(arg_keys[4], 1), SEQS * MICRO * SEQ_LEN // BLOCK)
    item_owner_turns = jax.random.permutation(jax.random.fold_in(arg_keys[4], 3), SEQS * MICRO * SEQ_LEN // BLOCK)
    item_owner = jax.vmap(lambda own, number: routed_block(jax.random.fold_in(arg_keys[4], 2), own, number, BLOCK, OWNERS, 1, ROW_CAP, 2))(item_owner_keys, item_owner_turns).reshape((SEQS, MICRO, SEQ_LEN, 1))
    item_slot = touch_ends(ranked(arg_keys[5], (SEQS, MICRO, SEQ_LEN), ROWS_OWN, 2), jax.random.fold_in(arg_keys[5], 3), 0, ROWS_OWN - 1).astype(jnp.int32)
    table = normal_values(arg_keys[6], (ROWS, D), 0.5, 4.0, ((0, 128),), jnp.float32)
    moment = normal_values(arg_keys[7], (ROWS, D), 0.3, 3.0, ((0, 128),), jnp.float32)
    second = jnp.clip(jnp.exp(math.log(1.0) - 4.6051702 * jax.random.uniform(arg_keys[8], (ROWS,), jnp.float32) ** block_scale(arg_keys[8], (ROWS,), ((0, 128),), -0.2, 0.2)), 0.01, 1.0)
    return {"saved_input": saved_input, "out_grad": out_grad, "w_in": w_in, "w_out": w_out, "item_owner": item_owner, "item_slot": item_slot, "table": table, "moment": moment, "second": second}


LN_EPS = 1e-05
BETA_ONE = 0.8
BETA_TWO = 0.9
STEP_SIZE = 0.05
ADAM_EPS = 1e-08

def contract(form, left, right):
    left, right = lax.optimization_barrier((left, right))
    return jnp.einsum(form, left.astype(jnp.float32), right.astype(jnp.float32))

def normalize(values):
    center = values - lax.optimization_barrier(jnp.mean(values, -1, keepdims=True))
    inverse = lax.rsqrt(lax.optimization_barrier(jnp.mean(center * center, -1, keepdims=True)) + LN_EPS)
    return (center * inverse, inverse)

def norm_back(grad_norm, normed, inverse):
    return inverse * (grad_norm - lax.optimization_barrier(jnp.mean(grad_norm, -1, keepdims=True)) - normed * lax.optimization_barrier(jnp.mean(grad_norm * normed, -1, keepdims=True)))

def silu_slope(values, sigmoid):
    return sigmoid * (1.0 + values * (1.0 - sigmoid))

def layer_back(layer_in, grad_top, weight_in, weight_out, head_count):
    batch, length, width = layer_in.shape
    head_size = width // head_count
    scale = head_size ** (-0.5)
    normed_in, inverse_in = normalize(layer_in.astype(jnp.float32))
    flat_in = normed_in.astype(jnp.bfloat16).reshape(batch * length, width)
    pre_act = jnp.dot(flat_in, weight_in, preferred_element_type=jnp.float32)
    pre_sig = jax.nn.sigmoid(pre_act)
    activ = lax.optimization_barrier((pre_act * pre_sig).astype(jnp.bfloat16))
    activ = activ.reshape(batch, length, 4, width)
    gates = activ[:, :, 0]
    values = activ[:, :, 1].reshape(batch, length, head_count, head_size)
    queries = activ[:, :, 2].reshape(batch, length, head_count, head_size)
    key_rows = activ[:, :, 3].reshape(batch, length, head_count, head_size)
    scores = contract('blhs,bmhs->bhlm', queries, key_rows) * scale
    causal = jnp.arange(length)[:, None] >= jnp.arange(length)[None, :]
    score_sig = jax.nn.sigmoid(scores)
    weights = jnp.where(causal, scores * score_sig, 0.0).astype(jnp.bfloat16)
    mixed = contract('bhlm,bmhs->blhs', weights, values).reshape(batch, length, width)
    normed_mix, inverse_mix = normalize(mixed)
    gate_vals = gates.astype(jnp.float32)
    hidden = (normed_mix * gate_vals).astype(jnp.bfloat16).reshape(batch * length, width)
    flat_top = grad_top.reshape(batch * length, width)
    grad_out = jnp.dot(hidden.T, flat_top, preferred_element_type=jnp.float32)
    grad_hidden = jnp.dot(flat_top, weight_out.T, preferred_element_type=jnp.float32).reshape(batch, length, width)
    grad_gate = grad_hidden * normed_mix
    grad_mix = norm_back(grad_hidden * gate_vals, normed_mix, inverse_mix).astype(jnp.bfloat16)
    grad_mix = grad_mix.reshape(batch, length, head_count, head_size)
    grad_weights = contract('blhs,bmhs->bhlm', grad_mix, values)
    grad_values = contract('bhlm,blhs->bmhs', weights, grad_mix)
    grad_scores = (jnp.where(causal, grad_weights * silu_slope(scores, score_sig), 0.0) * scale).astype(jnp.bfloat16)
    grad_queries = contract('bhlm,bmhs->blhs', grad_scores, key_rows)
    grad_keys = contract('bhlm,blhs->bmhs', grad_scores, queries)
    grad_act = jnp.stack([grad_gate, grad_values.reshape(batch, length, width), grad_queries.reshape(batch, length, width), grad_keys.reshape(batch, length, width)], 2)
    grad_act = grad_act.reshape(batch * length, 4 * width)
    grad_pre = (grad_act * silu_slope(pre_act, pre_sig)).astype(jnp.bfloat16)
    grad_in = jnp.dot(flat_in.T, grad_pre, preferred_element_type=jnp.float32)
    grad_normed = jnp.dot(grad_pre, weight_in.T, preferred_element_type=jnp.float32).reshape(batch, length, width)
    grad_below = norm_back(grad_normed, normed_in, inverse_in) + grad_top.astype(jnp.float32)
    return (grad_below.astype(jnp.bfloat16), grad_in, grad_out)

def reference(saved_input, out_grad, w_in, w_out, item_owner, item_slot, table, moment, second):
    acc_in = [jnp.zeros((D, 4 * D), jnp.float32) for layer_idx in range(LAYERS)]
    acc_out = [jnp.zeros((D, D), jnp.float32) for layer_idx in range(LAYERS)]
    firsts = []
    for micro_idx in range(MICRO):
        grad_top = out_grad[micro_idx]
        for layer_idx in reversed(range(LAYERS)):
            grad_top, part_in, part_out = layer_back(saved_input[layer_idx, micro_idx], grad_top, w_in[layer_idx], w_out[layer_idx], HEADS)
            acc_in[layer_idx] = acc_in[layer_idx] + part_in
            acc_out[layer_idx] = acc_out[layer_idx] + part_out
        firsts.append(grad_top)
    factor = TOKENS ** (-0.5)
    grad_in = jnp.stack(acc_in) * factor
    grad_out = jnp.stack(acc_out) * factor
    token_grads = jnp.stack(firsts, 1).reshape(-1, D).astype(jnp.float32)
    places = (item_owner[..., 0] * ROWS_OWN + item_slot).reshape(-1).astype(jnp.int32)
    row_grad = jax.ops.segment_sum(token_grads, places, num_segments=ROWS)
    hits = jax.ops.segment_sum(jnp.ones_like(places), places, num_segments=ROWS)
    touched = hits > 0
    moment_new = jnp.where(touched[:, None], BETA_ONE * moment + (1.0 - BETA_ONE) * row_grad, moment)
    second_new = jnp.where(touched, BETA_TWO * second + (1.0 - BETA_TWO) * lax.optimization_barrier(jnp.mean(row_grad * row_grad, -1)), second)
    table_new = jnp.where(touched[:, None], table - STEP_SIZE * moment_new / (jnp.sqrt(second_new)[:, None] + ADAM_EPS), table)
    return (grad_in, grad_out, table_new, moment_new, second_new)
```

```python
import functools

import jax
import jax.numpy as jnp
from jax import lax
from jax.experimental import pallas as pl
from jax.experimental.pallas import tpu as pltpu
from jax.sharding import PartitionSpec as P

HEADS = 4
BLOCK = 64
LN_EPS = 1e-05
BETA_ONE = 0.8
BETA_TWO = 0.9
STEP_SIZE = 0.05
ADAM_EPS = 1e-08

F32 = jnp.float32
BF = jnp.bfloat16
MESH = pl.DeviceIdType.MESH
PARTS = 5
LANES = 128


def mm(a, b):
    return jnp.dot(a, b, preferred_element_type=F32)


def mm_nt(a, b):
    return lax.dot_general(a, b, (((1,), (1,)), ((), ())), preferred_element_type=F32)


def sigmoid(v):
    return 0.5 + 0.5 * jnp.tanh(0.5 * v)


def mean(v):
    return jnp.mean(v, -1, keepdims=True)


def normed(v):
    center = v - mean(v)
    inverse = lax.rsqrt(mean(center * center) + LN_EPS)
    return center * inverse, inverse


def norm_back(grad, norm, inverse):
    return inverse * (grad - mean(grad) - norm * mean(grad * norm))


def slope(v, s):
    return s * (1.0 + v * (1.0 - s))


def kernel(
    dims,
    x_ref, og_ref, win_ref, wout_ref, owner_ref, slot_ref,
    rg_ref, hits_ref, gi_ref, go_ref,
    xn_s, rx_s, act_s, slope_s, w_s, zs_s, mn_s, rm_s,
    hx_s, hx_o, lt_s, g_s, below_s, d_s, d_r,
    gw_s, gx_r, gz_s, gz_r, f_s,
    p_s, tk_s, idp_s, idx_r, idz_s, idt_s, tp_s, tx_r, tz_s, tt_s, oh_s,
    hop_ss, hop_rs, hx_ss, hx_rs, d_ss, d_rs, gx_ss, gx_rs, gz_ss, gz_rs, f_ss, f_rs,
    tk_ss, tk_rs, ix_ss, ix_rs, iz_ss, iz_rs, ic_ss, ic_rs,
):
    ns, nz, nx, cap = dims
    micro, length, width = x_ref.shape
    half = width // 2
    hs = width // HEADS
    scale = hs ** (-0.5)
    rows = width // (nz * nx)
    own_rows = rg_ref.shape[0]
    piece = length // (nz * nx)
    sec = lax.axis_index("section")
    smp = lax.axis_index("sample")
    core = lax.axis_index("replica")
    zz, xx = lax.div(smp, nx), lax.rem(smp, nx)

    def wrap(v, n):
        return lax.rem(v, n)

    def x_peer(d):
        return (sec, zz * nx + wrap(xx + d, nx), core)

    def z_peer(d):
        return (sec, wrap(zz + d, nz) * nx + xx, core)

    other = (sec, smp, 1 - core)

    def remote(src, dst, ss, rs, dev):
        return pltpu.make_async_remote_copy(
            src_ref=src, dst_ref=dst, send_sem=ss, recv_sem=rs, device_id=dev, device_id_type=MESH
        )

    barrier = pltpu.get_barrier_semaphore()
    peers = [other]
    peers += [(wrap(sec + d, ns), smp, core) for d in range(1, ns)]
    peers += [x_peer(d) for d in range(1, nx)]
    peers += [z_peer(d) for d in range(1, nz)]
    for peer in peers:
        pl.semaphore_signal(barrier, inc=1, device_id=peer, device_id_type=MESH)

    row_id = lax.broadcasted_iota(jnp.int32, (length, length), 0)
    col_id = lax.broadcasted_iota(jnp.int32, (length, length), 1)

    def forward(m):
        xn, rx = normed(x_ref[m].astype(F32))
        xn_s[m] = xn
        rx_s[m] = rx
        xb = xn.astype(BF)
        hx_s[1, m] = xb
        for k in range(4):
            pre = mm(xb, win_ref[:, k * width:(k + 1) * width])
            s = sigmoid(pre)
            act_s[m, k] = (pre * s).astype(BF)
            slope_s[m, k] = slope(pre, s)
        causal = row_id >= col_id
        mixed = []
        for h in range(HEADS):
            cols = slice(h * hs, (h + 1) * hs)
            z = mm_nt(act_s[m, 2, :, cols], act_s[m, 3, :, cols]) * scale
            s = sigmoid(z)
            wt = jnp.where(causal, z * s, 0.0).astype(BF)
            w_s[m, h] = wt.T
            zs_s[m, h] = jnp.where(causal, slope(z, s), 0.0) * scale
            mixed.append(mm(wt, act_s[m, 1, :, cols]))
        mn, rm = normed(jnp.concatenate(mixed, -1))
        mn_s[m] = mn
        rm_s[m] = rm
        hx_s[0, m] = (mn * act_s[m, 0].astype(F32)).astype(BF)

    def keep(m, k, value):
        d_s[0, k, m] = value[:, :half]
        d_s[1, k, m] = value[:, half:]
        remote(d_s.at[1 - core, k, m], d_r.at[k, m], d_ss.at[k, m], d_rs.at[k, m], other).start()

    def backward(m):
        g = g_s[m]
        keep(m, 0, g)
        dh = mm_nt(g, wout_ref[...])
        mn = mn_s[m]
        dpre = [(dh * mn * slope_s[m, 0]).astype(BF)]
        keep(m, 1, dpre[0])
        dmix = norm_back(dh * act_s[m, 0].astype(F32), mn, rm_s[m]).astype(BF)
        dv, dq, dk = [], [], []
        for h in range(HEADS):
            cols = slice(h * hs, (h + 1) * hs)
            dm = dmix[:, cols]
            dw = mm_nt(dm, act_s[m, 1, :, cols])
            dv.append(mm(w_s[m, h], dm))
            dz = (dw * zs_s[m, h]).astype(BF)
            dq.append(mm(dz, act_s[m, 3, :, cols]))
            dk.append(mm(dz.T, act_s[m, 2, :, cols]))
        for k, part in enumerate((dv, dq, dk)):
            dpre.append((jnp.concatenate(part, -1) * slope_s[m, k + 1]).astype(BF))
            keep(m, k + 2, dpre[-1])
        dxn = mm_nt(dpre[0], win_ref[:, :width])
        for k in range(1, 4):
            dxn = dxn + mm_nt(dpre[k], win_ref[:, k * width:(k + 1) * width])
        below = norm_back(dxn, xn_s[m], rx_s[m]) + g.astype(F32)
        below_s[m] = below.astype(BF)

    def pack_plan(m):
        owner = owner_ref[m:m + 1, :]
        spread = jnp.broadcast_to(owner.astype(F32), (length, length))
        same = (spread == spread.T) & (lax.div(row_id, BLOCK) == lax.div(col_id, BLOCK)) & (row_id < col_id)
        rank = jnp.sum(jnp.where(same, 1.0, 0.0), 0, keepdims=True).astype(jnp.int32)
        place = owner - sec * (nz * nx)
        mine = (place >= 0) & (place < nz * nx)
        place = jnp.where(mine, place, 0)
        block = lax.div(lax.broadcasted_iota(jnp.int32, (1, length), 1), BLOCK)
        to = (lax.rem(place, nx) * nz + lax.div(place, nx)) * piece + block * cap + rank
        to = jnp.where(mine, to, -1)
        plan = jnp.where(row_id == to, 1.0, 0.0).astype(BF)
        p_s[m] = plan
        name = slot_ref[m:m + 1, :] + 1
        high, low = lax.div(name, 32), lax.rem(name, 32)
        both = jnp.where(row_id < length // 2, high, low).astype(F32).astype(BF)
        return mm_nt(plan, both).astype(BF)

    def x_start(pack, inbox, ss, rs):
        inbox[0] = pack[xx]
        for d in range(1, nx):
            remote(pack.at[wrap(xx + d, nx)], inbox.at[d], ss.at[d], rs.at[d], x_peer(d)).start()

    def z_start(inbox, outbox, total, xs, xr, ss, rs):
        for d in range(1, nx):
            remote(inbox.at[d], inbox.at[d], xs.at[d], xr.at[d], x_peer(d)).wait_recv()
        src = lax.div(lax.rem(row_id, nx * piece), piece) * (nz * piece)
        src = src + lax.div(row_id, nx * piece) * piece + lax.rem(row_id, piece)
        turn = jnp.where(src == col_id, 1.0, 0.0).astype(BF)
        stacked = inbox[...].reshape(length, inbox.shape[-1])
        moved = mm(turn, stacked).astype(BF)
        outbox[...] = moved.reshape(outbox.shape)
        total[0] = outbox[zz]
        for d in range(1, nz):
            remote(outbox.at[wrap(zz + d, nz)], total.at[d], ss.at[d], rs.at[d], z_peer(d)).start()

    def core_start(mine, zs, zr, ss, rs):
        for d in range(1, nz):
            remote(mine.at[d], mine.at[d], zs.at[d], zr.at[d], z_peer(d)).wait_recv()
        remote(mine, mine, ss, rs, other).start()

    def prepare():
        remote(hx_s, hx_o, hx_ss.at[0], hx_rs.at[0], other).start()
        ids = jnp.concatenate([pack_plan(m) for m in range(micro)], -1)
        idp_s[...] = ids.reshape(idp_s.shape)
        x_start(idp_s, idx_r, ix_ss.at[0], ix_rs.at[0])
        for kind in range(2):
            lt_s[kind, 0] = hx_s[kind].reshape(micro * length, width).T
        z_start(idx_r, idz_s, idt_s.at[core], ix_ss.at[0], ix_rs.at[0], iz_ss.at[0], iz_rs.at[0])
        remote(hx_s, hx_o, hx_ss.at[0], hx_rs.at[0], other).wait_recv()
        for kind in range(2):
            lt_s[kind, 1] = hx_o[kind].reshape(micro * length, width).T
        core_start(idt_s.at[core], iz_ss.at[0], iz_rs.at[0], ic_ss.at[0], ic_rs.at[0])
        remote(idt_s.at[1 - core], idt_s.at[1 - core], ic_ss.at[0], ic_rs.at[0], other).wait_recv()
        hits = jnp.zeros((own_rows, 1), F32)
        own_id = lax.broadcasted_iota(jnp.int32, (own_rows, length), 0).astype(F32)
        for c in range(2):
            for m in range(micro):
                both = idt_s[c, :, :, m * LANES:(m + 1) * LANES].reshape(length, LANES).astype(F32).T
                name = both[:1] * 32.0 + both[LANES // 2:LANES // 2 + 1] - 1.0
                hot = jnp.where(own_id == name, 1.0, 0.0)
                hits = hits + jnp.sum(hot, -1, keepdims=True)
                oh_s[:, (c * micro + m) * length:(c * micro + m + 1) * length] = hot.astype(BF)
        hits_ref[...] = jnp.broadcast_to(hits, hits_ref.shape)

    @pl.when(sec < ns - 1)
    def _():
        @pl.loop(0, micro)
        def _(m):
            forward(m)

    @pl.when(sec == ns - 1)
    def _():
        forward(0)

    pl.semaphore_wait(barrier, len(peers))

    early = ns // 2

    @pl.when(sec < early)
    def _():
        prepare()

    def hop(m):
        return remote(
            below_s.at[m], g_s.at[m], hop_ss.at[m], hop_rs.at[m],
            (wrap(sec + ns - 1, ns), smp, core),
        )

    def token(m, place):
        return remote(
            below_s.at[m], tk_s.at[m], tk_ss.at[m, place], tk_rs.at[m, 0],
            (1 if place == 0 else ns - 1, smp, core),
        )

    def token_on(m, place):
        span = pl.ds(place * (length // 2), length // 2)
        return remote(
            tk_s.at[m, span], tk_s.at[m, span], tk_ss.at[m, 0], tk_rs.at[m, place], (2, smp, core)
        )

    @pl.loop(0, micro)
    def _(m):
        @pl.when(sec == ns - 1)
        def _():
            @pl.when(m > 0)
            def _():
                forward(m)
            g_s[m] = og_ref[m]

        @pl.when(sec < ns - 1)
        def _():
            hop(m).wait_recv()

        backward(m)

        @pl.when(sec > 0)
        def _():
            hop(m).start()

        @pl.when(sec == 0)
        def _():
            tk_s[m] = below_s[m]
            token(m, 0).start()
            if ns > 2:
                token(m, 1).start()

    @pl.when(sec >= early)
    def _():
        prepare()

    @pl.loop(0, PARTS)
    def _(k):
        for m in range(micro):
            remote(d_s.at[1 - core, k, m], d_r.at[k, m], d_ss.at[k, m], d_rs.at[k, m], other).wait_recv()
        kind = jnp.minimum(k, 1)
        part = mm(lt_s[kind, 0], d_s[core, k].reshape(micro * length, half))
        part = part + mm(lt_s[kind, 1], d_r[k].reshape(micro * length, half))
        part = part.astype(BF)
        for z in range(nz):
            for x in range(nx):
                at = (z * nx + x) * rows
                gw_s[k, x, z * rows:(z + 1) * rows, :] = part[at:at + rows]
        for d in range(1, nx):
            remote(
                gw_s.at[k, wrap(xx + d, nx)], gx_r.at[k, d], gx_ss.at[k, d], gx_rs.at[k, d], x_peer(d)
            ).start()

    def get_tokens(m):
        if ns > 2:
            @pl.when((sec == 1) | (sec == 3))
            def _():
                token(m, 0).wait_recv()

            @pl.when(sec == 1)
            def _():
                token_on(m, 0).start()

            @pl.when(sec == 3)
            def _():
                token_on(m, 1).start()

            @pl.when(sec == 2)
            def _():
                token_on(m, 0).wait_recv()
                token_on(m, 1).wait_recv()
        else:
            @pl.when(sec == 1)
            def _():
                token(m, 0).wait_recv()
        packed = mm(p_s[m], tk_s[m]).astype(BF)
        tp_s[m] = packed.reshape(tp_s.shape[1:])
        x_start(tp_s.at[m], tx_r.at[m], ix_ss.at[1 + m], ix_rs.at[1 + m])

    get_tokens(0)

    @pl.when(sec == 0)
    def _():
        get_tokens(1)

    @pl.loop(0, PARTS)
    def _(k):
        total = gw_s[k, xx].astype(F32)
        for d in range(1, nx):
            remote(gx_r.at[k, d], gx_r.at[k, d], gx_ss.at[k, d], gx_rs.at[k, d], x_peer(d)).wait_recv()
            total = total + gx_r[k, d].astype(F32)
        total = total.astype(BF)
        for z in range(nz):
            gz_s[z, k] = total[z * rows:(z + 1) * rows]

    for d in range(1, nz):
        remote(gz_s.at[wrap(zz + d, nz)], gz_r.at[d], gz_ss.at[d], gz_rs.at[d], z_peer(d)).start()

    @pl.when(sec > 0)
    def _():
        get_tokens(1)

    for m in range(micro):
        z_start(
            tx_r.at[m], tz_s.at[m], tt_s.at[core, m],
            ix_ss.at[1 + m], ix_rs.at[1 + m], iz_ss.at[1 + m], iz_rs.at[1 + m],
        )

    total = gz_s[zz].astype(F32)
    for d in range(1, nz):
        remote(gz_r.at[d], gz_r.at[d], gz_ss.at[d], gz_rs.at[d], z_peer(d)).wait_recv()
        total = total + gz_r[d].astype(F32)
    f_s[core] = total.astype(BF)
    remote(f_s.at[core], f_s.at[core], f_ss.at[0], f_rs.at[0], other).start()

    for m in range(micro):
        core_start(tt_s.at[core, m], iz_ss.at[1 + m], iz_rs.at[1 + m], ic_ss.at[1 + m], ic_rs.at[1 + m])

    remote(f_s.at[1 - core], f_s.at[1 - core], f_ss.at[0], f_rs.at[0], other).wait_recv()
    tokens_all = micro * length * nz * nx * 2
    factor = float(tokens_all) ** (-0.5)
    for c in range(2):
        go_ref[:, c * half:(c + 1) * half] = f_s[c, 0].astype(F32) * factor
        for k in range(4):
            at = k * width + c * half
            gi_ref[:, at:at + half] = f_s[c, k + 1].astype(F32) * factor

    for m in range(micro):
        remote(
            tt_s.at[1 - core, m], tt_s.at[1 - core, m], ic_ss.at[1 + m], ic_rs.at[1 + m], other
        ).wait_recv()
    rg_ref[...] = mm(oh_s[...], tt_s[...].reshape(2 * micro * length, width))

    remote(hx_s, hx_o, hx_ss.at[0], hx_rs.at[0], other).wait_send()
    remote(f_s.at[core], f_s.at[core], f_ss.at[0], f_rs.at[0], other).wait_send()

    @pl.loop(0, PARTS)
    def _(k):
        for m in range(micro):
            remote(d_s.at[1 - core, k, m], d_r.at[k, m], d_ss.at[k, m], d_rs.at[k, m], other).wait_send()
        for d in range(1, nx):
            remote(
                gw_s.at[k, wrap(xx + d, nx)], gx_r.at[k, d], gx_ss.at[k, d], gx_rs.at[k, d], x_peer(d)
            ).wait_send()

    for d in range(1, nz):
        remote(gz_s.at[wrap(zz + d, nz)], gz_r.at[d], gz_ss.at[d], gz_rs.at[d], z_peer(d)).wait_send()
    for i in range(1 + micro):
        pack = idp_s if i == 0 else tp_s.at[i - 1]
        inbox = idx_r if i == 0 else tx_r.at[i - 1]
        outbox = idz_s if i == 0 else tz_s.at[i - 1]
        full = idt_s.at[core] if i == 0 else tt_s.at[core, i - 1]
        for d in range(1, nx):
            remote(
                pack.at[wrap(xx + d, nx)], inbox.at[d], ix_ss.at[i, d], ix_rs.at[i, d], x_peer(d)
            ).wait_send()
        for d in range(1, nz):
            remote(
                outbox.at[wrap(zz + d, nz)], full.at[d], iz_ss.at[i, d], iz_rs.at[i, d], z_peer(d)
            ).wait_send()
        remote(full, full, ic_ss.at[i], ic_rs.at[i], other).wait_send()
    for m in range(micro):
        @pl.when(sec > 0)
        def _():
            hop(m).wait_send()

        @pl.when(sec == 0)
        def _():
            token(m, 0).wait_send()
            if ns > 2:
                token(m, 1).wait_send()

        if ns > 2:
            @pl.when(sec == 1)
            def _():
                token_on(m, 0).wait_send()

            @pl.when(sec == 3)
            def _():
                token_on(m, 1).wait_send()


def exchange(dims, x, og, w_in, w_out, owner, slot, own_rows):
    ns, nz, nx, cap = dims
    micro, length, width = x.shape
    half = width // 2
    rows = width // (nz * nx)
    dma = pltpu.SemaphoreType.DMA
    vm = pltpu.VMEM
    lx, lz = length // nx, length // nz
    streams = 1 + micro
    wide = LANES * micro
    scratch = [
        vm((micro, length, width), F32),
        vm((micro, length, 1), F32),
        vm((micro, 4, length, width), BF),
        vm((micro, 4, length, width), F32),
        vm((micro, HEADS, length, length), BF),
        vm((micro, HEADS, length, length), F32),
        vm((micro, length, width), F32),
        vm((micro, length, 1), F32),
        vm((2, micro, length, width), BF),
        vm((2, micro, length, width), BF),
        vm((2, 2, width, micro * length), BF),
        vm((micro, length, width), BF),
        vm((micro, length, width), BF),
        vm((2, PARTS, micro, length, half), BF),
        vm((PARTS, micro, length, half), BF),
        vm((PARTS, nx, nz * rows, half), BF),
        vm((PARTS, nx, nz * rows, half), BF),
        vm((nz, PARTS, rows, half), BF),
        vm((nz, PARTS, rows, half), BF),
        vm((2, PARTS, rows, half), BF),
        vm((micro, length, length), BF),
        vm((micro, length, width), BF),
        vm((nx, lx, wide), BF),
        vm((nx, lx, wide), BF),
        vm((nz, lz, wide), BF),
        vm((2, nz, lz, wide), BF),
        vm((micro, nx, lx, width), BF),
        vm((micro, nx, lx, width), BF),
        vm((micro, nz, lz, width), BF),
        vm((2, micro, nz, lz, width), BF),
        vm((own_rows, 2 * micro * length), BF),
        dma((micro,)), dma((micro,)), dma((1,)), dma((1,)),
        dma((PARTS, micro)), dma((PARTS, micro)),
        dma((PARTS, nx)), dma((PARTS, nx)),
        dma((nz,)), dma((nz,)), dma((1,)), dma((1,)),
        dma((micro, 2)), dma((micro, 2)),
        dma((streams, nx)), dma((streams, nx)),
        dma((streams, nz)), dma((streams, nz)),
        dma((streams,)), dma((streams,)),
    ]
    return pl.pallas_call(
        functools.partial(kernel, dims),
        out_shape=(
            jax.ShapeDtypeStruct((own_rows, width), F32),
            jax.ShapeDtypeStruct((own_rows, LANES), F32),
            jax.ShapeDtypeStruct((rows, 4 * width), F32),
            jax.ShapeDtypeStruct((rows, width), F32),
        ),
        in_specs=[pl.BlockSpec(memory_space=pltpu.VMEM)] * 6,
        out_specs=[pl.BlockSpec(memory_space=pltpu.VMEM)] * 4,
        scratch_shapes=scratch,
        compiler_params=pltpu.CompilerParams(
            collective_id=0, has_side_effects=True, vmem_limit_bytes=48 << 20
        ),
    )(x, og, w_in, w_out, owner, slot)


def local(nz, nx, saved_input, out_grad, w_in, w_out, item_owner, item_slot, table, moment, second):
    ns = lax.axis_size("section")
    micro, length, width = out_grad.shape[0], out_grad.shape[2], out_grad.shape[3]
    owners = ns * nz * nx
    cap = max(2, 2 * BLOCK // owners)
    row_grad, hits, grad_in, grad_out = exchange(
        (ns, nz, nx, cap),
        saved_input[0, :, 0],
        out_grad[:, 0],
        w_in[0],
        w_out[0],
        item_owner.reshape(micro, length),
        item_slot.reshape(micro, length),
        table.shape[0],
    )
    hits = hits[:, 0]
    touched = hits > 0.5
    moment_new = jnp.where(
        touched[:, None], BETA_ONE * moment + (1.0 - BETA_ONE) * row_grad, moment
    )
    second_new = jnp.where(
        touched, BETA_TWO * second + (1.0 - BETA_TWO) * jnp.mean(row_grad * row_grad, -1), second
    )
    table_new = jnp.where(
        touched[:, None],
        table - STEP_SIZE * moment_new / (jnp.sqrt(second_new)[:, None] + ADAM_EPS),
        table,
    )
    return (grad_in[None], grad_out[None], table_new, moment_new, second_new)


def solution(mesh):
    samples = mesh.shape["sample"]
    nx = 4 if samples >= 16 else 2
    nz = samples // nx
    placed = (
        P("section", None, ("sample", "replica"), None, None),
        P(None, ("sample", "replica"), None, None),
        P("section", None, None),
        P("section", None, None),
        P(("sample", "replica"), None, None, None),
        P(("sample", "replica"), None, None),
        P(("section", "sample"), None),
        P(("section", "sample"), None),
        P(("section", "sample")),
    )
    return jax.shard_map(
        functools.partial(local, nz, nx),
        mesh=mesh,
        in_specs=placed,
        out_specs=(
            P("section", "sample", None),
            P("section", "sample", None),
            P(("section", "sample"), None),
            P(("section", "sample"), None),
            P(("section", "sample")),
        ),
        check_vma=False,
    )
```

```python
import functools

import jax
import jax.numpy as jnp
from jax import lax
from jax.experimental import pallas as pl
from jax.experimental.pallas import tpu as pltpu
from jax.sharding import PartitionSpec as P

HEADS = 4
BLOCK = 64
LN_EPS = 1e-05
BETA_ONE = 0.8
BETA_TWO = 0.9
STEP_SIZE = 0.05
ADAM_EPS = 1e-08

F32 = jnp.float32
BF = jnp.bfloat16
MESH = pl.DeviceIdType.MESH
PARTS = 5
LANES = 128


def mm(a, b):
    return jnp.dot(a, b, preferred_element_type=F32)


def mm_nt(a, b):
    return lax.dot_general(a, b, (((1,), (1,)), ((), ())), preferred_element_type=F32)


def sigmoid(v):
    return 0.5 + 0.5 * jnp.tanh(0.5 * v)


def mean(v):
    return jnp.mean(v, -1, keepdims=True)


def normed(v):
    center = v - mean(v)
    inverse = lax.rsqrt(mean(center * center) + LN_EPS)
    return center * inverse, inverse


def norm_back(grad, norm, inverse):
    return inverse * (grad - mean(grad) - norm * mean(grad * norm))


def slope(v, s):
    return s * (1.0 + v * (1.0 - s))


def kernel(
    dims,
    x_hbm, og_hbm, win_hbm, wout_hbm, owner_hbm, slot_hbm,
    rg_hbm, hits_hbm, f_hbm,
    rg_ref, hits_ref, x_ref, win_ref, wout_ref, owner_ref, slot_ref,
    xn_s, rx_s, act_s, slope_s, w_s, zs_s, mn_s, rm_s,
    hx_s, hx_o, lt_s, g_s, below_s, d_s, d_r,
    gw_s, g1_r, g2_s, g2_r, gz_s, gz_r, f_s,
    p_s, tk_s, idp_s, idx_r, idz_s, idt_s, tp_s, tx_r, tz_s, tt_s, oh_s,
    in_ss, out_ss, hop_ss, hop_rs, hx_ss, hx_rs, d_ss, d_rs,
    g1_ss, g1_rs, g2_ss, g2_rs, gz_ss, gz_rs, f_ss, f_rs,
    tk_ss, tk_rs, ix_ss, ix_rs, iz_ss, iz_rs, ic_ss, ic_rs,
):
    ns, nz, nx, cap = dims
    micro, length, width = x_ref.shape
    half = width // 2
    hs = width // HEADS
    scale = hs ** (-0.5)
    rows = width // (nz * nx)
    own_rows = rg_hbm.shape[0]
    piece = length // (nz * nx)
    sec = lax.axis_index("section")
    smp = lax.axis_index("sample")
    core = lax.axis_index("replica")
    zz, xx = lax.div(smp, nx), lax.rem(smp, nx)

    def wrap(v, n):
        return lax.rem(v, n)

    def x_peer(d):
        return (sec, zz * nx + wrap(xx + d, nx), core)

    def z_peer(d):
        return (sec, wrap(zz + d, nz) * nx + xx, core)

    other = (sec, smp, 1 - core)

    def remote(src, dst, ss, rs, dev):
        return pltpu.make_async_remote_copy(
            src_ref=src, dst_ref=dst, send_sem=ss, recv_sem=rs, device_id=dev, device_id_type=MESH
        )

    def load(i, src, dst):
        return pltpu.make_async_copy(src, dst, in_ss.at[i])

    def save(i, src, dst):
        return pltpu.make_async_copy(src, dst, out_ss.at[i])

    def save_rows(b):
        at = pl.ds(b * LANES, LANES)
        return save(2 + b, rg_ref.at[at], rg_hbm.at[at])

    loads = [
        load(i, src, dst)
        for i, (src, dst) in enumerate((
            (x_hbm, x_ref), (win_hbm, win_ref), (wout_hbm, wout_ref),
            (owner_hbm, owner_ref), (slot_hbm, slot_ref),
        ))
    ]
    for one in loads:
        one.start()

    @pl.when(sec == ns - 1)
    def _():
        load(5, og_hbm, g_s).start()

    barrier = pltpu.get_barrier_semaphore()
    peers = [other]
    peers += [(wrap(sec + d, ns), smp, core) for d in range(1, ns)]
    peers += [x_peer(d) for d in range(1, nx)]
    peers += [z_peer(d) for d in range(1, nz)]
    for peer in peers:
        pl.semaphore_signal(barrier, inc=1, device_id=peer, device_id_type=MESH)

    row_id = lax.broadcasted_iota(jnp.int32, (length, length), 0)
    col_id = lax.broadcasted_iota(jnp.int32, (length, length), 1)

    def forward(m):
        xn, rx = normed(x_ref[m].astype(F32))
        xn_s[m] = xn
        rx_s[m] = rx
        xb = xn.astype(BF)
        hx_s[1, m] = xb
        for k in range(4):
            pre = mm(xb, win_ref[:, k * width:(k + 1) * width])
            s = sigmoid(pre)
            act_s[m, k] = (pre * s).astype(BF)
            slope_s[m, k] = slope(pre, s)
        causal = row_id >= col_id
        mixed = []
        for h in range(HEADS):
            cols = slice(h * hs, (h + 1) * hs)
            z = mm_nt(act_s[m, 2, :, cols], act_s[m, 3, :, cols]) * scale
            s = sigmoid(z)
            wt = jnp.where(causal, z * s, 0.0).astype(BF)
            w_s[m, h] = wt.T
            zs_s[m, h] = jnp.where(causal, slope(z, s), 0.0) * scale
            mixed.append(mm(wt, act_s[m, 1, :, cols]))
        mn, rm = normed(jnp.concatenate(mixed, -1))
        mn_s[m] = mn
        rm_s[m] = rm
        hx_s[0, m] = (mn * act_s[m, 0].astype(F32)).astype(BF)

    first = jnp.where(core == 0, 1, nx - 1)
    second = nx - first

    def flip(v, mask):
        pair = v + 1 - 2 * lax.rem(v, 2)
        return jnp.where(mask == 1, pair, nx - 1 - v)

    def x_at(x):
        return (sec, zz * nx + x, core)

    def g1_copy(k):
        return remote(
            gw_s.at[k, pl.ds(2, 2)], g1_r.at[k], g1_ss.at[k], g1_rs.at[k], x_at(flip(xx, first))
        )

    def g2_copy(k):
        return remote(g2_s.at[k], g2_r.at[k], g2_ss.at[k], g2_rs.at[k], x_at(flip(xx, second)))

    def gz_copy(k, d):
        return remote(
            gz_s.at[wrap(zz + d, nz), k], gz_r.at[d, k], gz_ss.at[d, k], gz_rs.at[d, k], z_peer(d)
        )

    def d_copy(k, m):
        return remote(d_s.at[1 - core, k, m], d_r.at[k, m], d_ss.at[k, m], d_rs.at[k, m], other)

    def gradient(k, kind):
        for m in range(micro):
            d_copy(k, m).wait_recv()
        part = mm(lt_s[kind, 0], d_s[core, k].reshape(micro * length, half))
        part = part + mm(lt_s[kind, 1], d_r[k].reshape(micro * length, half))
        part = part.astype(BF)
        for x in range(nx):
            slot = jnp.where(
                xx == x, 0, jnp.where(flip(xx, second) == x, 1, jnp.where(flip(xx, first) == x, 2, 3))
            )
            for z in range(nz):
                at = (z * nx + x) * rows
                gw_s[k, slot, z * rows:(z + 1) * rows, :] = part[at:at + rows]
        g1_copy(k).start()

    def keep(m, k, value):
        d_s[0, k, m] = value[:, :half]
        d_s[1, k, m] = value[:, half:]
        d_copy(k, m).start()

    def backward(m):
        g = g_s[m]
        keep(m, 0, g)
        dh = mm_nt(g, wout_ref[...])
        mn = mn_s[m]
        dpre = [(dh * mn * slope_s[m, 0]).astype(BF)]
        keep(m, 1, dpre[0])
        dmix = norm_back(dh * act_s[m, 0].astype(F32), mn, rm_s[m]).astype(BF)
        dv, dq, dk = [], [], []
        for h in range(HEADS):
            cols = slice(h * hs, (h + 1) * hs)
            dm = dmix[:, cols]
            dw = mm_nt(dm, act_s[m, 1, :, cols])
            dv.append(mm(w_s[m, h], dm))
            dz = (dw * zs_s[m, h]).astype(BF)
            dq.append(mm(dz, act_s[m, 3, :, cols]))
            dk.append(mm(dz.T, act_s[m, 2, :, cols]))
        for k, part in enumerate((dv, dq, dk)):
            dpre.append((jnp.concatenate(part, -1) * slope_s[m, k + 1]).astype(BF))
            keep(m, k + 2, dpre[-1])

        @pl.when((sec == 0) & (m == micro - 1))
        def _():
            gradient(0, 0)
            gradient(1, 1)

        dxn = mm_nt(dpre[0], win_ref[:, :width])
        for k in range(1, 4):
            dxn = dxn + mm_nt(dpre[k], win_ref[:, k * width:(k + 1) * width])
        below = norm_back(dxn, xn_s[m], rx_s[m]) + g.astype(F32)
        below_s[m] = below.astype(BF)

    def pack_plan(m):
        owner = owner_ref[m:m + 1, :]
        spread = jnp.broadcast_to(owner.astype(F32), (length, length))
        same = (spread == spread.T) & (lax.div(row_id, BLOCK) == lax.div(col_id, BLOCK)) & (row_id < col_id)
        rank = jnp.sum(jnp.where(same, 1.0, 0.0), 0, keepdims=True).astype(jnp.int32)
        place = owner - sec * (nz * nx)
        mine = (place >= 0) & (place < nz * nx)
        place = jnp.where(mine, place, 0)
        block = lax.div(lax.broadcasted_iota(jnp.int32, (1, length), 1), BLOCK)
        to = (lax.rem(place, nx) * nz + lax.div(place, nx)) * piece + block * cap + rank
        to = jnp.where(mine, to, -1)
        plan = jnp.where(row_id == to, 1.0, 0.0).astype(BF)
        p_s[m] = plan
        name = slot_ref[m:m + 1, :] + 1
        high, low = lax.div(name, 32), lax.rem(name, 32)
        both = jnp.where(row_id < length // 2, high, low).astype(F32).astype(BF)
        return mm_nt(plan, both).astype(BF)

    def x_start(pack, inbox, ss, rs):
        inbox[0] = pack[xx]
        for d in range(1, nx):
            remote(pack.at[wrap(xx + d, nx)], inbox.at[d], ss.at[d], rs.at[d], x_peer(d)).start()

    def z_start(inbox, outbox, total, xs, xr, ss, rs):
        for d in range(1, nx):
            remote(inbox.at[d], inbox.at[d], xs.at[d], xr.at[d], x_peer(d)).wait_recv()
        src = lax.div(lax.rem(row_id, nx * piece), piece) * (nz * piece)
        src = src + lax.div(row_id, nx * piece) * piece + lax.rem(row_id, piece)
        turn = jnp.where(src == col_id, 1.0, 0.0).astype(BF)
        stacked = inbox[...].reshape(length, inbox.shape[-1])
        moved = mm(turn, stacked).astype(BF)
        outbox[...] = moved.reshape(outbox.shape)
        total[0] = outbox[zz]
        for d in range(1, nz):
            remote(outbox.at[wrap(zz + d, nz)], total.at[d], ss.at[d], rs.at[d], z_peer(d)).start()

    def core_start(mine, zs, zr, ss, rs):
        for d in range(1, nz):
            remote(mine.at[d], mine.at[d], zs.at[d], zr.at[d], z_peer(d)).wait_recv()
        remote(mine, mine, ss, rs, other).start()

    def prepare():
        remote(hx_s, hx_o, hx_ss.at[0], hx_rs.at[0], other).start()
        ids = jnp.concatenate([pack_plan(m) for m in range(micro)], -1)
        idp_s[...] = ids.reshape(idp_s.shape)
        x_start(idp_s, idx_r, ix_ss.at[0], ix_rs.at[0])
        for kind in range(2):
            lt_s[kind, 0] = hx_s[kind].reshape(micro * length, width).T
        z_start(idx_r, idz_s, idt_s.at[core], ix_ss.at[0], ix_rs.at[0], iz_ss.at[0], iz_rs.at[0])
        remote(hx_s, hx_o, hx_ss.at[0], hx_rs.at[0], other).wait_recv()
        for kind in range(2):
            lt_s[kind, 1] = hx_o[kind].reshape(micro * length, width).T
        core_start(idt_s.at[core], iz_ss.at[0], iz_rs.at[0], ic_ss.at[0], ic_rs.at[0])
        remote(idt_s.at[1 - core], idt_s.at[1 - core], ic_ss.at[0], ic_rs.at[0], other).wait_recv()
        hits = jnp.zeros((own_rows, 1), F32)
        own_id = lax.broadcasted_iota(jnp.int32, (own_rows, length), 0).astype(F32)
        for c in range(2):
            for m in range(micro):
                both = idt_s[c, :, :, m * LANES:(m + 1) * LANES].reshape(length, LANES).astype(F32).T
                name = both[:1] * 32.0 + both[LANES // 2:LANES // 2 + 1] - 1.0
                hot = jnp.where(own_id == name, 1.0, 0.0)
                hits = hits + jnp.sum(hot, -1, keepdims=True)
                oh_s[:, (c * micro + m) * length:(c * micro + m + 1) * length] = hot.astype(BF)
        for b in range(own_rows // LANES):
            column = hits[b * LANES:(b + 1) * LANES]
            hits_ref[b:b + 1, :] = jnp.broadcast_to(column, (LANES, LANES)).T[:1]
        save(0, hits_ref, hits_hbm).start()

    loads[0].wait()
    loads[1].wait()

    @pl.when(sec < ns - 1)
    def _():
        @pl.loop(0, micro)
        def _(m):
            forward(m)

    @pl.when(sec == ns - 1)
    def _():
        forward(0)

    for one in loads[2:]:
        one.wait()

    @pl.when(sec == ns - 1)
    def _():
        load(5, og_hbm, g_s).wait()

    pl.semaphore_wait(barrier, len(peers))

    early = ns // 2

    @pl.when(sec < early)
    def _():
        prepare()

    def hop(m):
        return remote(
            below_s.at[m], g_s.at[m], hop_ss.at[m], hop_rs.at[m],
            (wrap(sec + ns - 1, ns), smp, core),
        )

    def token(m, place):
        return remote(
            below_s.at[m], tk_s.at[m], tk_ss.at[m, place], tk_rs.at[m, 0],
            (1 if place == 0 else ns - 1, smp, core),
        )

    def token_on(m, place):
        span = pl.ds(place * (length // 2), length // 2)
        return remote(
            tk_s.at[m, span], tk_s.at[m, span], tk_ss.at[m, 0], tk_rs.at[m, place], (2, smp, core)
        )

    def pack(m):
        packed = mm(p_s[m], tk_s[m]).astype(BF)
        tp_s[m] = packed.reshape(tp_s.shape[1:])
        x_start(tp_s.at[m], tx_r.at[m], ix_ss.at[1 + m], ix_rs.at[1 + m])

    @pl.loop(0, micro)
    def _(m):
        @pl.when((sec == ns - 1) & (m > 0))
        def _():
            forward(m)

        @pl.when(sec < ns - 1)
        def _():
            hop(m).wait_recv()

        backward(m)

        @pl.when(sec > 0)
        def _():
            hop(m).start()

        @pl.when(sec == 0)
        def _():
            tk_s[m] = below_s[m]
            token(m, 0).start()
            if ns > 2:
                token(m, 1).start()
            pack(m)

    @pl.when(sec >= early)
    def _():
        prepare()

    @pl.loop(jnp.where(sec == 0, 2, 0), PARTS)
    def _(k):
        gradient(k, jnp.minimum(k, 1))

    def get_tokens(m):
        if ns > 2:
            @pl.when((sec == 1) | (sec == 3))
            def _():
                token(m, 0).wait_recv()

            @pl.when(sec == 1)
            def _():
                token_on(m, 0).start()

            @pl.when(sec == 3)
            def _():
                token_on(m, 1).start()

            @pl.when(sec == 2)
            def _():
                token_on(m, 0).wait_recv()
                token_on(m, 1).wait_recv()
        else:
            token(m, 0).wait_recv()
        pack(m)

    def by_section(at_zero, at_one, at_rest):
        return jnp.where(sec == 0, at_zero, jnp.where(sec == 1, at_one, at_rest))

    def on_step(step, places, action):
        start = [by_section(*place) for place in places]

        @pl.when((step == start[0]) | (step == start[1]))
        def _():
            action(jnp.where(step == start[1], 1, 0))

    @pl.loop(0, 11)
    def _(step):
        @pl.when(step < PARTS)
        def _():
            g1_copy(step).wait_recv()
            total = gw_s[step, 1].astype(F32) + g1_r[step, 1].astype(F32)
            g2_s[step] = total.astype(BF)
            g2_copy(step).start()

        @pl.when((step > 0) & (step <= PARTS))
        def _():
            k = step - 1
            g2_copy(k).wait_recv()
            total = gw_s[k, 0].astype(F32) + g1_r[k, 0].astype(F32) + g2_r[k].astype(F32)
            total = total.astype(BF)
            for z in range(nz):
                gz_s[z, k] = total[z * rows:(z + 1) * rows]
            for d in range(1, nz):
                gz_copy(k, d).start()

        on_step(step, ((-1, 2, 5), (-1, 5, 7)), get_tokens)
        on_step(
            step, ((1, 3, 6), (2, 6, 8)),
            lambda m: z_start(
                tx_r.at[m], tz_s.at[m], tt_s.at[core, m],
                ix_ss.at[1 + m], ix_rs.at[1 + m], iz_ss.at[1 + m], iz_rs.at[1 + m],
            ),
        )
        on_step(
            step, ((4, 7, 9), (5, 8, 10)),
            lambda m: core_start(
                tt_s.at[core, m], iz_ss.at[1 + m], iz_rs.at[1 + m], ic_ss.at[1 + m], ic_rs.at[1 + m]
            ),
        )

    total = gz_s[zz].astype(F32)
    for d in range(1, nz):
        for k in range(PARTS):
            gz_copy(k, d).wait_recv()
        total = total + gz_r[d].astype(F32)
    f_s[core] = total.astype(BF)
    remote(f_s.at[core], f_s.at[core], f_ss.at[0], f_rs.at[0], other).start()

    for m in range(micro):
        remote(
            tt_s.at[1 - core, m], tt_s.at[1 - core, m], ic_ss.at[1 + m], ic_rs.at[1 + m], other
        ).wait_recv()
    tokens = tt_s[...].reshape(2 * micro * length, width)
    for b in range(own_rows // LANES):
        at = slice(b * LANES, (b + 1) * LANES)
        rg_ref[at, :] = mm(oh_s[at, :], tokens)
        save_rows(b).start()
    remote(f_s.at[1 - core], f_s.at[1 - core], f_ss.at[0], f_rs.at[0], other).wait_recv()
    save(1, f_s, f_hbm).start()

    remote(hx_s, hx_o, hx_ss.at[0], hx_rs.at[0], other).wait_send()
    remote(f_s.at[core], f_s.at[core], f_ss.at[0], f_rs.at[0], other).wait_send()

    @pl.loop(0, PARTS)
    def _(k):
        for m in range(micro):
            d_copy(k, m).wait_send()
        g1_copy(k).wait_send()
        g2_copy(k).wait_send()
        for d in range(1, nz):
            gz_copy(k, d).wait_send()

    for i in range(1 + micro):
        pack_from = idp_s if i == 0 else tp_s.at[i - 1]
        inbox = idx_r if i == 0 else tx_r.at[i - 1]
        outbox = idz_s if i == 0 else tz_s.at[i - 1]
        full = idt_s.at[core] if i == 0 else tt_s.at[core, i - 1]
        for d in range(1, nx):
            remote(
                pack_from.at[wrap(xx + d, nx)], inbox.at[d], ix_ss.at[i, d], ix_rs.at[i, d], x_peer(d)
            ).wait_send()
        for d in range(1, nz):
            remote(
                outbox.at[wrap(zz + d, nz)], full.at[d], iz_ss.at[i, d], iz_rs.at[i, d], z_peer(d)
            ).wait_send()
        remote(full, full, ic_ss.at[i], ic_rs.at[i], other).wait_send()
    for m in range(micro):
        @pl.when(sec > 0)
        def _():
            hop(m).wait_send()

        @pl.when(sec == 0)
        def _():
            token(m, 0).wait_send()
            if ns > 2:
                token(m, 1).wait_send()

        if ns > 2:
            @pl.when(sec == 1)
            def _():
                token_on(m, 0).wait_send()

            @pl.when(sec == 3)
            def _():
                token_on(m, 1).wait_send()

    save(0, hits_ref, hits_hbm).wait()
    save(1, f_s, f_hbm).wait()
    for b in range(own_rows // LANES):
        save_rows(b).wait()


def finish(
    factor,
    rg_hbm, hits_hbm, f_hbm, table_in, moment_in, second_in,
    gi_hbm, go_hbm, table_hbm, moment_hbm, second_hbm,
    rg_ref, hits_ref, f_ref, table_ref, moment_ref, second_ref, gi_s, go_s, table_s, moment_s, second_s, in_sems, sems,
):
    half = f_ref.shape[-1]
    width = 2 * half
    blocks = rg_ref.shape[0] // LANES

    copies = []

    loads = [
        pltpu.make_async_copy(src, dst, in_sems.at[i])
        for i, (src, dst) in enumerate(((hits_hbm, hits_ref), (second_in, second_ref), (f_hbm, f_ref)))
    ]

    def row_loads(b):
        at = pl.ds(b * LANES, LANES)
        pairs = ((rg_hbm, rg_ref), (moment_in, moment_ref), (table_in, table_ref))
        return [
            pltpu.make_async_copy(src.at[at], dst.at[at], in_sems.at[3 + 3 * b + i])
            for i, (src, dst) in enumerate(pairs)
        ]

    loads[0].start()
    loads[1].start()
    for b in range(blocks):
        for load in row_loads(b):
            load.start()
    loads[2].start()
    loads[0].wait()
    loads[1].wait()

    def put(src, dst):
        copy = pltpu.make_async_copy(src, dst, sems.at[len(copies)])
        copy.start()
        copies.append(copy)

    for b in range(blocks):
        at = pl.ds(b * LANES, LANES)
        for load in row_loads(b):
            load.wait()
        grad = rg_ref[at, :]
        hit = jnp.broadcast_to(hits_ref[b:b + 1, :], (LANES, LANES)).T > 0.5
        wide = jnp.concatenate([hit] * (width // LANES), -1)
        square = jnp.mean(grad * grad, -1, keepdims=True)
        square = jnp.broadcast_to(square, (LANES, LANES))
        old = jnp.broadcast_to(second_ref[b:b + 1, :], (LANES, LANES)).T
        new = jnp.where(hit, BETA_TWO * old + (1.0 - BETA_TWO) * square, old)
        second_s[b:b + 1, :] = new.T[:1]
        old_moment = moment_ref[at, :]
        moment = jnp.where(wide, BETA_ONE * old_moment + (1.0 - BETA_ONE) * grad, old_moment)
        moment_s[at, :] = moment
        put(moment_s.at[at], moment_hbm.at[at])
        old_table = table_ref[at, :]
        below = jnp.concatenate([jnp.sqrt(new) + ADAM_EPS] * (width // LANES), -1)
        table_s[at, :] = jnp.where(wide, old_table - STEP_SIZE * moment / below, old_table)
        put(table_s.at[at], table_hbm.at[at])
    put(second_s, second_hbm)
    loads[2].wait()
    for c in range(2):
        go_s[:, c * half:(c + 1) * half] = f_ref[c, 0].astype(F32) * factor
        for k in range(4):
            at = k * width + c * half
            gi_s[:, at:at + half] = f_ref[c, k + 1].astype(F32) * factor
    put(go_s, go_hbm)
    put(gi_s, gi_hbm)
    for copy in copies:
        copy.wait()


def exchange(dims, x, og, w_in, w_out, owner, slot, own_rows):
    ns, nz, nx, cap = dims
    micro, length, width = x.shape
    half = width // 2
    rows = width // (nz * nx)
    dma = pltpu.SemaphoreType.DMA
    vm = pltpu.VMEM
    lx, lz = length // nx, length // nz
    streams = 1 + micro
    wide = LANES * micro
    scratch = [
        vm((own_rows, width), F32),
        vm((own_rows // LANES, LANES), F32),
        vm((micro, length, width), BF),
        vm((width, 4 * width), BF),
        vm((width, width), BF),
        vm((micro, length), jnp.int32),
        vm((micro, length), jnp.int32),
        vm((micro, length, width), F32),
        vm((micro, length, 1), F32),
        vm((micro, 4, length, width), BF),
        vm((micro, 4, length, width), F32),
        vm((micro, HEADS, length, length), BF),
        vm((micro, HEADS, length, length), F32),
        vm((micro, length, width), F32),
        vm((micro, length, 1), F32),
        vm((2, micro, length, width), BF),
        vm((2, micro, length, width), BF),
        vm((2, 2, width, micro * length), BF),
        vm((micro, length, width), BF),
        vm((micro, length, width), BF),
        vm((2, PARTS, micro, length, half), BF),
        vm((PARTS, micro, length, half), BF),
        vm((PARTS, nx, nz * rows, half), BF),
        vm((PARTS, 2, nz * rows, half), BF),
        vm((PARTS, nz * rows, half), BF),
        vm((PARTS, nz * rows, half), BF),
        vm((nz, PARTS, rows, half), BF),
        vm((nz, PARTS, rows, half), BF),
        vm((2, PARTS, rows, half), BF),
        vm((micro, length, length), BF),
        vm((micro, length, width), BF),
        vm((nx, lx, wide), BF),
        vm((nx, lx, wide), BF),
        vm((nz, lz, wide), BF),
        vm((2, nz, lz, wide), BF),
        vm((micro, nx, lx, width), BF),
        vm((micro, nx, lx, width), BF),
        vm((micro, nz, lz, width), BF),
        vm((2, micro, nz, lz, width), BF),
        vm((own_rows, 2 * micro * length), BF),
        dma((6,)), dma((2 + own_rows // LANES,)), dma((micro,)), dma((micro,)), dma((1,)), dma((1,)),
        dma((PARTS, micro)), dma((PARTS, micro)),
        dma((PARTS,)), dma((PARTS,)), dma((PARTS,)), dma((PARTS,)),
        dma((nz, PARTS)), dma((nz, PARTS)), dma((1,)), dma((1,)),
        dma((micro, 2)), dma((micro, 2)),
        dma((streams, nx)), dma((streams, nx)),
        dma((streams, nz)), dma((streams, nz)),
        dma((streams,)), dma((streams,)),
    ]
    return pl.pallas_call(
        functools.partial(kernel, dims),
        out_shape=(
            jax.ShapeDtypeStruct((own_rows, width), F32),
            jax.ShapeDtypeStruct((own_rows // LANES, LANES), F32),
            jax.ShapeDtypeStruct((2, PARTS, rows, half), BF),
        ),
        in_specs=[pl.BlockSpec(memory_space=pltpu.HBM)] * 6,
        out_specs=[pl.BlockSpec(memory_space=pltpu.HBM)] * 3,
        scratch_shapes=scratch,
        compiler_params=pltpu.CompilerParams(
            collective_id=0, has_side_effects=True, vmem_limit_bytes=56 << 20
        ),
    )(x, og, w_in, w_out, owner, slot)


def local(nz, nx, saved_input, out_grad, w_in, w_out, item_owner, item_slot, table, moment, second):
    ns = lax.axis_size("section")
    micro, length, width = out_grad.shape[0], out_grad.shape[2], out_grad.shape[3]
    owners = ns * nz * nx
    cap = max(2, 2 * BLOCK // owners)
    own_rows = table.shape[0]
    rows = width // (nz * nx)
    row_grad, hits, grads = exchange(
        (ns, nz, nx, cap),
        saved_input[0, :, 0],
        out_grad[:, 0],
        w_in[0],
        w_out[0],
        item_owner.reshape(micro, length),
        item_slot.reshape(micro, length),
        own_rows,
    )
    tokens = micro * length * nz * nx * lax.axis_size("replica")
    lines = (own_rows // LANES, LANES)
    shapes = [(rows, 4 * width), (rows, width), (own_rows, width), (own_rows, width), lines]
    grad_in, grad_out, table_new, moment_new, second_new = pl.pallas_call(
        functools.partial(finish, float(tokens) ** (-0.5)),
        out_shape=[jax.ShapeDtypeStruct(shape, F32) for shape in shapes],
        in_specs=[pl.BlockSpec(memory_space=pltpu.HBM)] * 6,
        out_specs=[pl.BlockSpec(memory_space=pltpu.HBM)] * 5,
        scratch_shapes=[pltpu.VMEM(part.shape, part.dtype) for part in (row_grad, hits, grads)]
        + [pltpu.VMEM(shape, F32) for shape in shapes[2:]]
        + [pltpu.VMEM(shape, F32) for shape in shapes]
        + [pltpu.SemaphoreType.DMA((3 + 3 * lines[0],)), pltpu.SemaphoreType.DMA((2 * lines[0] + 3,))],
        compiler_params=pltpu.CompilerParams(vmem_limit_bytes=56 << 20),
    )(row_grad, hits, grads, table, moment, second.reshape(lines))
    return (grad_in[None], grad_out[None], table_new, moment_new, second_new.reshape(own_rows))


def solution(mesh):
    nx = 4
    nz = mesh.shape["sample"] // nx
    placed = (
        P("section", None, ("sample", "replica"), None, None),
        P(None, ("sample", "replica"), None, None),
        P("section", None, None),
        P("section", None, None),
        P(("sample", "replica"), None, None, None),
        P(("sample", "replica"), None, None),
        P(("section", "sample"), None),
        P(("section", "sample"), None),
        P(("section", "sample")),
    )
    return jax.shard_map(
        functools.partial(local, nz, nx),
        mesh=mesh,
        in_specs=placed,
        out_specs=(
            P("section", "sample", None),
            P("section", "sample", None),
            P(("section", "sample"), None),
            P(("section", "sample"), None),
            P(("section", "sample")),
        ),
        check_vma=False,
    )
```

```python
import functools

import jax
import jax.numpy as jnp
from jax import lax
from jax.experimental import pallas as pl
from jax.experimental.pallas import tpu as pltpu
from jax.sharding import PartitionSpec as P

HEADS = 4
BLOCK = 64
LN_EPS = 1e-05
BETA_ONE = 0.8
BETA_TWO = 0.9
STEP_SIZE = 0.05
ADAM_EPS = 1e-08

F32 = jnp.float32
BF = jnp.bfloat16
MESH = pl.DeviceIdType.MESH
PARTS = 5
LANES = 128
LAG = 2


def mm(a, b):
    return jnp.dot(a, b, preferred_element_type=F32)


def mm_nt(a, b):
    return lax.dot_general(a, b, (((1,), (1,)), ((), ())), preferred_element_type=F32)


def sigmoid(v):
    return 0.5 + 0.5 * jnp.tanh(0.5 * v)


def mean(v):
    return jnp.mean(v, -1, keepdims=True)


def normed(v):
    center = v - mean(v)
    inverse = lax.rsqrt(mean(center * center) + LN_EPS)
    return center * inverse, inverse


def norm_back(grad, norm, inverse):
    return inverse * (grad - mean(grad) - norm * mean(grad * norm))


def slope(v, s):
    return s * (1.0 + v * (1.0 - s))


def kernel(
    dims,
    x_hbm, og_hbm, win_hbm, wout_hbm, owner_hbm, slot_hbm,
    rg_hbm, hits_hbm, f_hbm,
    rg_ref, hits_ref, x_ref, win_ref, wout_ref, owner_ref, slot_ref,
    xn_s, rx_s, act_s, slope_s, w_s, zs_s, mn_s, rm_s,
    hx_s, hx_o, lt_s, g_s, below_s, d_s, d_r,
    gw_s, g1_r, g2_s, g2_r, gz_s, gz_r, f_s,
    p_s, tk_s, idp_s, idx_r, idz_s, idt_s, tp_s, tx_r, tz_s, tt_s, oh_s,
    in_ss, out_ss, hop_ss, hop_rs, hx_ss, hx_rs, d_ss, d_rs,
    g1_ss, g1_rs, g2_ss, g2_rs, gz_ss, gz_rs, f_ss, f_rs,
    tk_ss, tk_rs, ix_ss, ix_rs, iz_ss, iz_rs, ic_ss, ic_rs,
):
    ns, nz, nx, cap = dims
    micro, length, width = x_ref.shape
    half = width // 2
    hs = width // HEADS
    scale = hs ** (-0.5)
    rows = width // (nz * nx)
    own_rows = rg_hbm.shape[0]
    piece = length // (nz * nx)
    sec = lax.axis_index("section")
    smp = lax.axis_index("sample")
    core = lax.axis_index("replica")
    zz, xx = lax.div(smp, nx), lax.rem(smp, nx)

    def wrap(v, n):
        return lax.rem(v, n)

    def x_peer(d):
        return (sec, zz * nx + wrap(xx + d, nx), core)

    def z_peer(d):
        return (sec, wrap(zz + d, nz) * nx + xx, core)

    other = (sec, smp, 1 - core)

    def remote(src, dst, ss, rs, dev):
        return pltpu.make_async_remote_copy(
            src_ref=src, dst_ref=dst, send_sem=ss, recv_sem=rs, device_id=dev, device_id_type=MESH
        )

    def load(i, src, dst):
        return pltpu.make_async_copy(src, dst, in_ss.at[i])

    def save(i, src, dst):
        return pltpu.make_async_copy(src, dst, out_ss.at[i])

    def save_rows(b):
        at = pl.ds(b * LANES, LANES)
        return save(2 + b, rg_ref.at[at], rg_hbm.at[at])

    loads = [
        load(i, src, dst)
        for i, (src, dst) in enumerate((
            (x_hbm, x_ref), (win_hbm, win_ref), (wout_hbm, wout_ref),
            (owner_hbm, owner_ref), (slot_hbm, slot_ref),
        ))
    ]
    for one in loads:
        one.start()

    @pl.when(sec == ns - 1)
    def _():
        load(5, og_hbm, g_s).start()

    barrier = pltpu.get_barrier_semaphore()
    peers = [other]
    peers += [(wrap(sec + d, ns), smp, core) for d in range(1, ns)]
    peers += [x_peer(d) for d in range(1, nx)]
    peers += [z_peer(d) for d in range(1, nz)]
    for peer in peers:
        pl.semaphore_signal(barrier, inc=1, device_id=peer, device_id_type=MESH)

    row_id = lax.broadcasted_iota(jnp.int32, (length, length), 0)
    col_id = lax.broadcasted_iota(jnp.int32, (length, length), 1)

    def forward(m):
        xn, rx = normed(x_ref[m].astype(F32))
        xn_s[m] = xn
        rx_s[m] = rx
        xb = xn.astype(BF)
        hx_s[1, m] = xb
        for k in range(4):
            pre = mm(xb, win_ref[:, k * width:(k + 1) * width])
            s = sigmoid(pre)
            act_s[m, k] = (pre * s).astype(BF)
            slope_s[m, k] = slope(pre, s)
        causal = row_id >= col_id
        mixed = []
        for h in range(HEADS):
            cols = slice(h * hs, (h + 1) * hs)
            z = mm_nt(act_s[m, 2, :, cols], act_s[m, 3, :, cols]) * scale
            s = sigmoid(z)
            wt = jnp.where(causal, z * s, 0.0).astype(BF)
            w_s[m, h] = wt.T
            zs_s[m, h] = jnp.where(causal, slope(z, s), 0.0) * scale
            mixed.append(mm(wt, act_s[m, 1, :, cols]))
        mn, rm = normed(jnp.concatenate(mixed, -1))
        mn_s[m] = mn
        rm_s[m] = rm
        hx_s[0, m] = (mn * act_s[m, 0].astype(F32)).astype(BF)

    first = jnp.where(core == 0, 1, nx - 1)
    second = nx - first

    def flip(v, mask):
        pair = v + 1 - 2 * lax.rem(v, 2)
        return jnp.where(mask == 1, pair, nx - 1 - v)

    def x_at(x):
        return (sec, zz * nx + x, core)

    def g1_copy(k):
        return remote(
            gw_s.at[k, pl.ds(2, 2)], g1_r.at[k], g1_ss.at[k], g1_rs.at[k], x_at(flip(xx, first))
        )

    def g2_copy(k):
        return remote(g2_s.at[k], g2_r.at[k], g2_ss.at[k], g2_rs.at[k], x_at(flip(xx, second)))

    def gz_copy(k, d):
        return remote(
            gz_s.at[wrap(zz + d, nz), k], gz_r.at[d, k], gz_ss.at[d, k], gz_rs.at[d, k], z_peer(d)
        )

    def d_copy(k, m):
        return remote(d_s.at[1 - core, k, m], d_r.at[k, m], d_ss.at[k, m], d_rs.at[k, m], other)

    def gradient(k, kind):
        for m in range(micro):
            d_copy(k, m).wait_recv()
        part = mm(lt_s[kind, 0], d_s[core, k].reshape(micro * length, half))
        part = part + mm(lt_s[kind, 1], d_r[k].reshape(micro * length, half))
        part = part.astype(BF)
        for x in range(nx):
            slot = jnp.where(
                xx == x, 0, jnp.where(flip(xx, second) == x, 1, jnp.where(flip(xx, first) == x, 2, 3))
            )
            for z in range(nz):
                at = (z * nx + x) * rows
                gw_s[k, slot, z * rows:(z + 1) * rows, :] = part[at:at + rows]
        g1_copy(k).start()

    def keep(m, k, value):
        d_s[0, k, m] = value[:, :half]
        d_s[1, k, m] = value[:, half:]
        d_copy(k, m).start()

    def backward(m):
        g = g_s[m]
        keep(m, 0, g)
        dh = mm_nt(g, wout_ref[...])
        mn = mn_s[m]
        dpre = [(dh * mn * slope_s[m, 0]).astype(BF)]
        keep(m, 1, dpre[0])
        dmix = norm_back(dh * act_s[m, 0].astype(F32), mn, rm_s[m]).astype(BF)
        dv, dq, dk = [], [], []
        for h in range(HEADS):
            cols = slice(h * hs, (h + 1) * hs)
            dm = dmix[:, cols]
            dw = mm_nt(dm, act_s[m, 1, :, cols])
            dv.append(mm(w_s[m, h], dm))
            dz = (dw * zs_s[m, h]).astype(BF)
            dq.append(mm(dz, act_s[m, 3, :, cols]))
            dk.append(mm(dz.T, act_s[m, 2, :, cols]))
        for k, part in enumerate((dv, dq, dk)):
            dpre.append((jnp.concatenate(part, -1) * slope_s[m, k + 1]).astype(BF))
            keep(m, k + 2, dpre[-1])

        @pl.when((sec == 0) & (m == micro - 1))
        def _():
            gradient(0, 0)
            gradient(1, 1)

        dxn = mm_nt(dpre[0], win_ref[:, :width])
        for k in range(1, 4):
            dxn = dxn + mm_nt(dpre[k], win_ref[:, k * width:(k + 1) * width])
        below = norm_back(dxn, xn_s[m], rx_s[m]) + g.astype(F32)
        below_s[m] = below.astype(BF)

    def pack_plan(m):
        owner = owner_ref[m:m + 1, :]
        spread = jnp.broadcast_to(owner.astype(F32), (length, length))
        same = (spread == spread.T) & (lax.div(row_id, BLOCK) == lax.div(col_id, BLOCK)) & (row_id < col_id)
        rank = jnp.sum(jnp.where(same, 1.0, 0.0), 0, keepdims=True).astype(jnp.int32)
        place = owner - sec * (nz * nx)
        mine = (place >= 0) & (place < nz * nx)
        place = jnp.where(mine, place, 0)
        block = lax.div(lax.broadcasted_iota(jnp.int32, (1, length), 1), BLOCK)
        to = (lax.rem(place, nx) * nz + lax.div(place, nx)) * piece + block * cap + rank
        to = jnp.where(mine, to, -1)
        plan = jnp.where(row_id == to, 1.0, 0.0).astype(BF)
        p_s[m] = plan
        name = slot_ref[m:m + 1, :] + 1
        high, low = lax.div(name, 32), lax.rem(name, 32)
        both = jnp.where(row_id < length // 2, high, low).astype(F32).astype(BF)
        return mm_nt(plan, both).astype(BF)

    def x_start(pack, inbox, ss, rs):
        inbox[0] = pack[xx]
        for d in range(1, nx):
            remote(pack.at[wrap(xx + d, nx)], inbox.at[d], ss.at[d], rs.at[d], x_peer(d)).start()

    def z_start(inbox, outbox, total, xs, xr, ss, rs):
        for d in range(1, nx):
            remote(inbox.at[d], inbox.at[d], xs.at[d], xr.at[d], x_peer(d)).wait_recv()
        src = lax.div(lax.rem(row_id, nx * piece), piece) * (nz * piece)
        src = src + lax.div(row_id, nx * piece) * piece + lax.rem(row_id, piece)
        turn = jnp.where(src == col_id, 1.0, 0.0).astype(BF)
        stacked = inbox[...].reshape(length, inbox.shape[-1])
        moved = mm(turn, stacked).astype(BF)
        outbox[...] = moved.reshape(outbox.shape)
        total[0] = outbox[zz]
        for d in range(1, nz):
            remote(outbox.at[wrap(zz + d, nz)], total.at[d], ss.at[d], rs.at[d], z_peer(d)).start()

    def core_start(mine, zs, zr, ss, rs):
        for d in range(1, nz):
            remote(mine.at[d], mine.at[d], zs.at[d], zr.at[d], z_peer(d)).wait_recv()
        remote(mine, mine, ss, rs, other).start()

    def prepare():
        remote(hx_s, hx_o, hx_ss.at[0], hx_rs.at[0], other).start()
        ids = jnp.concatenate([pack_plan(m) for m in range(micro)], -1)
        idp_s[...] = ids.reshape(idp_s.shape)
        x_start(idp_s, idx_r, ix_ss.at[0], ix_rs.at[0])
        for kind in range(2):
            lt_s[kind, 0] = hx_s[kind].reshape(micro * length, width).T
        z_start(idx_r, idz_s, idt_s.at[core], ix_ss.at[0], ix_rs.at[0], iz_ss.at[0], iz_rs.at[0])
        remote(hx_s, hx_o, hx_ss.at[0], hx_rs.at[0], other).wait_recv()
        for kind in range(2):
            lt_s[kind, 1] = hx_o[kind].reshape(micro * length, width).T
        core_start(idt_s.at[core], iz_ss.at[0], iz_rs.at[0], ic_ss.at[0], ic_rs.at[0])
        remote(idt_s.at[1 - core], idt_s.at[1 - core], ic_ss.at[0], ic_rs.at[0], other).wait_recv()
        hits = jnp.zeros((own_rows, 1), F32)
        own_id = lax.broadcasted_iota(jnp.int32, (own_rows, length), 0).astype(F32)
        for c in range(2):
            for m in range(micro):
                both = idt_s[c, :, :, m * LANES:(m + 1) * LANES].reshape(length, LANES).astype(F32).T
                name = both[:1] * 32.0 + both[LANES // 2:LANES // 2 + 1] - 1.0
                hot = jnp.where(own_id == name, 1.0, 0.0)
                hits = hits + jnp.sum(hot, -1, keepdims=True)
                oh_s[:, (c * micro + m) * length:(c * micro + m + 1) * length] = hot.astype(BF)
        for b in range(own_rows // LANES):
            column = hits[b * LANES:(b + 1) * LANES]
            hits_ref[b:b + 1, :] = jnp.broadcast_to(column, (LANES, LANES)).T[:1]
        save(0, hits_ref, hits_hbm).start()

    loads[0].wait()
    loads[1].wait()

    @pl.when(sec < ns - 1)
    def _():
        @pl.loop(0, micro)
        def _(m):
            forward(m)

    @pl.when(sec == ns - 1)
    def _():
        forward(0)

    for one in loads[2:]:
        one.wait()

    @pl.when(sec == ns - 1)
    def _():
        load(5, og_hbm, g_s).wait()

    pl.semaphore_wait(barrier, len(peers))

    early = ns // 2

    @pl.when(sec < early)
    def _():
        prepare()

    def hop(m):
        return remote(
            below_s.at[m], g_s.at[m], hop_ss.at[m], hop_rs.at[m],
            (wrap(sec + ns - 1, ns), smp, core),
        )

    def token(m, place):
        return remote(
            below_s.at[m], tk_s.at[m], tk_ss.at[m, place], tk_rs.at[m, 0],
            (1 if place == 0 else ns - 1, smp, core),
        )

    def token_on(m, place):
        span = pl.ds(place * (length // 2), length // 2)
        return remote(
            tk_s.at[m, span], tk_s.at[m, span], tk_ss.at[m, 0], tk_rs.at[m, place], (2, smp, core)
        )

    def pack(m):
        packed = mm(p_s[m], tk_s[m]).astype(BF)
        tp_s[m] = packed.reshape(tp_s.shape[1:])
        x_start(tp_s.at[m], tx_r.at[m], ix_ss.at[1 + m], ix_rs.at[1 + m])

    @pl.loop(0, micro)
    def _(m):
        @pl.when((sec == ns - 1) & (m > 0))
        def _():
            forward(m)

        @pl.when(sec < ns - 1)
        def _():
            hop(m).wait_recv()

        backward(m)

        @pl.when(sec > 0)
        def _():
            hop(m).start()

        @pl.when(sec == 0)
        def _():
            tk_s[m] = below_s[m]
            token(m, 0).start()
            if ns > 2:
                token(m, 1).start()
            pack(m)

    @pl.when(sec >= early)
    def _():
        prepare()

    def get_tokens(m):
        if ns > 2:
            @pl.when((sec == 1) | (sec == 3))
            def _():
                token(m, 0).wait_recv()

            @pl.when(sec == 1)
            def _():
                token_on(m, 0).start()

            @pl.when(sec == 3)
            def _():
                token_on(m, 1).start()

            @pl.when(sec == 2)
            def _():
                token_on(m, 0).wait_recv()
                token_on(m, 1).wait_recv()
        else:
            token(m, 0).wait_recv()
        pack(m)

    def by_section(places):
        at = jnp.int32(places[-1])
        for number in range(len(places) - 2, -1, -1):
            at = jnp.where(sec == number, places[number], at)
        return at

    def on_step(step, places, action):
        start = [by_section(place) for place in places]

        @pl.when((step == start[0]) | (step == start[1]))
        def _():
            action(jnp.where(step == start[1], 1, 0))

    @pl.loop(jnp.where(sec == 0, 2, 0), 10)
    def _(step):
        @pl.when(step < PARTS)
        def _():
            gradient(step, jnp.minimum(step, 1))

        @pl.when((step >= LAG) & (step < PARTS + LAG))
        def _():
            k = step - LAG
            g1_copy(k).wait_recv()
            total = gw_s[k, 1].astype(F32) + g1_r[k, 1].astype(F32)
            g2_s[k] = total.astype(BF)
            g2_copy(k).start()

        @pl.when((step > LAG) & (step <= PARTS + LAG))
        def _():
            k = step - LAG - 1
            g2_copy(k).wait_recv()
            total = gw_s[k, 0].astype(F32) + g1_r[k, 0].astype(F32) + g2_r[k].astype(F32)
            total = total.astype(BF)
            for z in range(nz):
                gz_s[z, k] = total[z * rows:(z + 1) * rows]
            for d in range(1, nz):
                gz_copy(k, d).start()

        on_step(step, ((-1, 4, 5, 6), (-1, 5, 6, 7)), get_tokens)
        on_step(
            step, ((2, 5, 6, 7), (4, 7, 8, 8)),
            lambda m: z_start(
                tx_r.at[m], tz_s.at[m], tt_s.at[core, m],
                ix_ss.at[1 + m], ix_rs.at[1 + m], iz_ss.at[1 + m], iz_rs.at[1 + m],
            ),
        )
        on_step(
            step, ((4, 7, 8, 8), (6, 8, 9, 9)),
            lambda m: core_start(
                tt_s.at[core, m], iz_ss.at[1 + m], iz_rs.at[1 + m], ic_ss.at[1 + m], ic_rs.at[1 + m]
            ),
        )

    total = gz_s[zz].astype(F32)
    for d in range(1, nz):
        for k in range(PARTS):
            gz_copy(k, d).wait_recv()
        total = total + gz_r[d].astype(F32)
    f_s[core] = total.astype(BF)
    remote(f_s.at[core], f_s.at[core], f_ss.at[0], f_rs.at[0], other).start()

    for m in range(micro):
        remote(
            tt_s.at[1 - core, m], tt_s.at[1 - core, m], ic_ss.at[1 + m], ic_rs.at[1 + m], other
        ).wait_recv()
    tokens = tt_s[...].reshape(2 * micro * length, width)
    for b in range(own_rows // LANES):
        at = slice(b * LANES, (b + 1) * LANES)
        rg_ref[at, :] = mm(oh_s[at, :], tokens)
        save_rows(b).start()
    remote(f_s.at[1 - core], f_s.at[1 - core], f_ss.at[0], f_rs.at[0], other).wait_recv()
    save(1, f_s, f_hbm).start()

    remote(hx_s, hx_o, hx_ss.at[0], hx_rs.at[0], other).wait_send()
    remote(f_s.at[core], f_s.at[core], f_ss.at[0], f_rs.at[0], other).wait_send()

    @pl.loop(0, PARTS)
    def _(k):
        for m in range(micro):
            d_copy(k, m).wait_send()
        g1_copy(k).wait_send()
        g2_copy(k).wait_send()
        for d in range(1, nz):
            gz_copy(k, d).wait_send()

    for i in range(1 + micro):
        pack_from = idp_s if i == 0 else tp_s.at[i - 1]
        inbox = idx_r if i == 0 else tx_r.at[i - 1]
        outbox = idz_s if i == 0 else tz_s.at[i - 1]
        full = idt_s.at[core] if i == 0 else tt_s.at[core, i - 1]
        for d in range(1, nx):
            remote(
                pack_from.at[wrap(xx + d, nx)], inbox.at[d], ix_ss.at[i, d], ix_rs.at[i, d], x_peer(d)
            ).wait_send()
        for d in range(1, nz):
            remote(
                outbox.at[wrap(zz + d, nz)], full.at[d], iz_ss.at[i, d], iz_rs.at[i, d], z_peer(d)
            ).wait_send()
        remote(full, full, ic_ss.at[i], ic_rs.at[i], other).wait_send()
    for m in range(micro):
        @pl.when(sec > 0)
        def _():
            hop(m).wait_send()

        @pl.when(sec == 0)
        def _():
            token(m, 0).wait_send()
            if ns > 2:
                token(m, 1).wait_send()

        if ns > 2:
            @pl.when(sec == 1)
            def _():
                token_on(m, 0).wait_send()

            @pl.when(sec == 3)
            def _():
                token_on(m, 1).wait_send()

    save(0, hits_ref, hits_hbm).wait()
    save(1, f_s, f_hbm).wait()
    for b in range(own_rows // LANES):
        save_rows(b).wait()


def finish(
    factor,
    rg_hbm, hits_hbm, f_hbm, table_in, moment_in, second_in,
    gi_hbm, go_hbm, table_hbm, moment_hbm, second_hbm,
    rg_ref, hits_ref, f_ref, table_ref, moment_ref, second_ref, gi_s, go_s, table_s, moment_s, second_s, in_sems, sems,
):
    half = f_ref.shape[-1]
    width = 2 * half
    blocks = rg_ref.shape[0] // LANES

    copies = []

    loads = [
        pltpu.make_async_copy(src, dst, in_sems.at[i])
        for i, (src, dst) in enumerate(((hits_hbm, hits_ref), (second_in, second_ref), (f_hbm, f_ref)))
    ]

    def row_loads(b):
        at = pl.ds(b * LANES, LANES)
        pairs = ((rg_hbm, rg_ref), (moment_in, moment_ref), (table_in, table_ref))
        return [
            pltpu.make_async_copy(src.at[at], dst.at[at], in_sems.at[3 + 3 * b + i])
            for i, (src, dst) in enumerate(pairs)
        ]

    loads[0].start()
    loads[1].start()
    for b in range(blocks):
        for load in row_loads(b):
            load.start()
    loads[2].start()
    loads[0].wait()
    loads[1].wait()

    def put(src, dst):
        copy = pltpu.make_async_copy(src, dst, sems.at[len(copies)])
        copy.start()
        copies.append(copy)

    for b in range(blocks):
        at = pl.ds(b * LANES, LANES)
        for load in row_loads(b):
            load.wait()
        grad = rg_ref[at, :]
        hit = jnp.broadcast_to(hits_ref[b:b + 1, :], (LANES, LANES)).T > 0.5
        wide = jnp.concatenate([hit] * (width // LANES), -1)
        square = jnp.mean(grad * grad, -1, keepdims=True)
        square = jnp.broadcast_to(square, (LANES, LANES))
        old = jnp.broadcast_to(second_ref[b:b + 1, :], (LANES, LANES)).T
        new = jnp.where(hit, BETA_TWO * old + (1.0 - BETA_TWO) * square, old)
        second_s[b:b + 1, :] = new.T[:1]
        old_moment = moment_ref[at, :]
        moment = jnp.where(wide, BETA_ONE * old_moment + (1.0 - BETA_ONE) * grad, old_moment)
        moment_s[at, :] = moment
        put(moment_s.at[at], moment_hbm.at[at])
        old_table = table_ref[at, :]
        below = jnp.concatenate([jnp.sqrt(new) + ADAM_EPS] * (width // LANES), -1)
        table_s[at, :] = jnp.where(wide, old_table - STEP_SIZE * moment / below, old_table)
        put(table_s.at[at], table_hbm.at[at])
    put(second_s, second_hbm)
    loads[2].wait()
    for c in range(2):
        go_s[:, c * half:(c + 1) * half] = f_ref[c, 0].astype(F32) * factor
        for k in range(4):
            at = k * width + c * half
            gi_s[:, at:at + half] = f_ref[c, k + 1].astype(F32) * factor
    put(go_s, go_hbm)
    put(gi_s, gi_hbm)
    for copy in copies:
        copy.wait()


def exchange(dims, x, og, w_in, w_out, owner, slot, own_rows):
    ns, nz, nx, cap = dims
    micro, length, width = x.shape
    half = width // 2
    rows = width // (nz * nx)
    dma = pltpu.SemaphoreType.DMA
    vm = pltpu.VMEM
    lx, lz = length // nx, length // nz
    streams = 1 + micro
    wide = LANES * micro
    scratch = [
        vm((own_rows, width), F32),
        vm((own_rows // LANES, LANES), F32),
        vm((micro, length, width), BF),
        vm((width, 4 * width), BF),
        vm((width, width), BF),
        vm((micro, length), jnp.int32),
        vm((micro, length), jnp.int32),
        vm((micro, length, width), F32),
        vm((micro, length, 1), F32),
        vm((micro, 4, length, width), BF),
        vm((micro, 4, length, width), F32),
        vm((micro, HEADS, length, length), BF),
        vm((micro, HEADS, length, length), F32),
        vm((micro, length, width), F32),
        vm((micro, length, 1), F32),
        vm((2, micro, length, width), BF),
        vm((2, micro, length, width), BF),
        vm((2, 2, width, micro * length), BF),
        vm((micro, length, width), BF),
        vm((micro, length, width), BF),
        vm((2, PARTS, micro, length, half), BF),
        vm((PARTS, micro, length, half), BF),
        vm((PARTS, nx, nz * rows, half), BF),
        vm((PARTS, 2, nz * rows, half), BF),
        vm((PARTS, nz * rows, half), BF),
        vm((PARTS, nz * rows, half), BF),
        vm((nz, PARTS, rows, half), BF),
        vm((nz, PARTS, rows, half), BF),
        vm((2, PARTS, rows, half), BF),
        vm((micro, length, length), BF),
        vm((micro, length, width), BF),
        vm((nx, lx, wide), BF),
        vm((nx, lx, wide), BF),
        vm((nz, lz, wide), BF),
        vm((2, nz, lz, wide), BF),
        vm((micro, nx, lx, width), BF),
        vm((micro, nx, lx, width), BF),
        vm((micro, nz, lz, width), BF),
        vm((2, micro, nz, lz, width), BF),
        vm((own_rows, 2 * micro * length), BF),
        dma((6,)), dma((2 + own_rows // LANES,)), dma((micro,)), dma((micro,)), dma((1,)), dma((1,)),
        dma((PARTS, micro)), dma((PARTS, micro)),
        dma((PARTS,)), dma((PARTS,)), dma((PARTS,)), dma((PARTS,)),
        dma((nz, PARTS)), dma((nz, PARTS)), dma((1,)), dma((1,)),
        dma((micro, 2)), dma((micro, 2)),
        dma((streams, nx)), dma((streams, nx)),
        dma((streams, nz)), dma((streams, nz)),
        dma((streams,)), dma((streams,)),
    ]
    return pl.pallas_call(
        functools.partial(kernel, dims),
        out_shape=(
            jax.ShapeDtypeStruct((own_rows, width), F32),
            jax.ShapeDtypeStruct((own_rows // LANES, LANES), F32),
            jax.ShapeDtypeStruct((2, PARTS, rows, half), BF),
        ),
        in_specs=[pl.BlockSpec(memory_space=pltpu.HBM)] * 6,
        out_specs=[pl.BlockSpec(memory_space=pltpu.HBM)] * 3,
        scratch_shapes=scratch,
        compiler_params=pltpu.CompilerParams(
            collective_id=0, has_side_effects=True, vmem_limit_bytes=56 << 20
        ),
    )(x, og, w_in, w_out, owner, slot)


def local(nz, nx, saved_input, out_grad, w_in, w_out, item_owner, item_slot, table, moment, second):
    ns = lax.axis_size("section")
    micro, length, width = out_grad.shape[0], out_grad.shape[2], out_grad.shape[3]
    owners = ns * nz * nx
    cap = max(2, 2 * BLOCK // owners)
    own_rows = table.shape[0]
    rows = width // (nz * nx)
    row_grad, hits, grads = exchange(
        (ns, nz, nx, cap),
        saved_input[0, :, 0],
        out_grad[:, 0],
        w_in[0],
        w_out[0],
        item_owner.reshape(micro, length),
        item_slot.reshape(micro, length),
        own_rows,
    )
    tokens = micro * length * nz * nx * lax.axis_size("replica")
    lines = (own_rows // LANES, LANES)
    shapes = [(rows, 4 * width), (rows, width), (own_rows, width), (own_rows, width), lines]
    grad_in, grad_out, table_new, moment_new, second_new = pl.pallas_call(
        functools.partial(finish, float(tokens) ** (-0.5)),
        out_shape=[jax.ShapeDtypeStruct(shape, F32) for shape in shapes],
        in_specs=[pl.BlockSpec(memory_space=pltpu.HBM)] * 6,
        out_specs=[pl.BlockSpec(memory_space=pltpu.HBM)] * 5,
        scratch_shapes=[pltpu.VMEM(part.shape, part.dtype) for part in (row_grad, hits, grads)]
        + [pltpu.VMEM(shape, F32) for shape in shapes[2:]]
        + [pltpu.VMEM(shape, F32) for shape in shapes]
        + [pltpu.SemaphoreType.DMA((3 + 3 * lines[0],)), pltpu.SemaphoreType.DMA((2 * lines[0] + 3,))],
        compiler_params=pltpu.CompilerParams(vmem_limit_bytes=56 << 20),
    )(row_grad, hits, grads, table, moment, second.reshape(lines))
    return (grad_in[None], grad_out[None], table_new, moment_new, second_new.reshape(own_rows))


def solution(mesh):
    nx = 4
    nz = mesh.shape["sample"] // nx
    placed = (
        P("section", None, ("sample", "replica"), None, None),
        P(None, ("sample", "replica"), None, None),
        P("section", None, None),
        P("section", None, None),
        P(("sample", "replica"), None, None, None),
        P(("sample", "replica"), None, None),
        P(("section", "sample"), None),
        P(("section", "sample"), None),
        P(("section", "sample")),
    )
    return jax.shard_map(
        functools.partial(local, nz, nx),
        mesh=mesh,
        in_specs=placed,
        out_specs=(
            P("section", "sample", None),
            P("section", "sample", None),
            P(("section", "sample"), None),
            P(("section", "sample"), None),
            P(("section", "sample")),
        ),
        check_vma=False,
    )
```

```python
import functools

import jax
import jax.numpy as jnp
from jax import lax
from jax.experimental import pallas as pl
from jax.experimental.pallas import tpu as pltpu
from jax.sharding import PartitionSpec as P

HEADS = 4
BLOCK = 64
LN_EPS = 1e-05
BETA_ONE = 0.8
BETA_TWO = 0.9
STEP_SIZE = 0.05
ADAM_EPS = 1e-08

F32 = jnp.float32
BF = jnp.bfloat16
MESH = pl.DeviceIdType.MESH
PARTS = 5
LANES = 128
LAG = 2


def mm(a, b):
    return jnp.dot(a, b, preferred_element_type=F32)


def mm_nt(a, b):
    return lax.dot_general(a, b, (((1,), (1,)), ((), ())), preferred_element_type=F32)


def sigmoid(v):
    return 0.5 + 0.5 * jnp.tanh(0.5 * v)


def mean(v):
    return jnp.mean(v, -1, keepdims=True)


def normed(v):
    center = v - mean(v)
    inverse = lax.rsqrt(mean(center * center) + LN_EPS)
    return center * inverse, inverse


def norm_back(grad, norm, inverse):
    return inverse * (grad - mean(grad) - norm * mean(grad * norm))


def slope(v, s):
    return s * (1.0 + v * (1.0 - s))


def kernel(
    dims,
    x_hbm, og_hbm, win_hbm, wout_hbm, owner_hbm, slot_hbm,
    oh_hbm, tt_hbm, hits_hbm, f_hbm,
    hits_ref, x_ref, win_ref, wout_ref, owner_ref, slot_ref,
    wint_s, woutt_s, vt_s, xn_s, rx_s, act_s, slope_s, w_s, zs_s, mn_s, rm_s,
    hx_s, hx_o, lt_s, g_s, below_s, d_s, d_r,
    gw_s, g1_r, g2_s, g2_r, gz_s, gz_r, f_s,
    p_s, tk_s, idp_s, idx_r, idz_s, idt_s, tp_s, tx_r, tz_s, tt_s, oh_s,
    in_ss, out_ss, hop_ss, hop_rs, hx_ss, hx_rs, d_ss, d_rs,
    g1_ss, g1_rs, g2_ss, g2_rs, gz_ss, gz_rs, f_ss, f_rs,
    tk_ss, tk_rs, ix_ss, ix_rs, iz_ss, iz_rs, ic_ss, ic_rs,
):
    ns, nz, nx, cap = dims
    micro, length, width = x_ref.shape
    half = width // 2
    mid = length // 2
    hs = width // HEADS
    scale = hs ** (-0.5)
    rows = width // (nz * nx)
    own_rows = oh_hbm.shape[0]
    piece = length // (nz * nx)
    sec = lax.axis_index("section")
    smp = lax.axis_index("sample")
    core = lax.axis_index("replica")
    zz, xx = lax.div(smp, nx), lax.rem(smp, nx)

    def wrap(v, n):
        return lax.rem(v, n)

    def x_peer(d):
        return (sec, zz * nx + wrap(xx + d, nx), core)

    def z_peer(d):
        return (sec, wrap(zz + d, nz) * nx + xx, core)

    other = (sec, smp, 1 - core)

    def remote(src, dst, ss, rs, dev):
        return pltpu.make_async_remote_copy(
            src_ref=src, dst_ref=dst, send_sem=ss, recv_sem=rs, device_id=dev, device_id_type=MESH
        )

    def load(i, src, dst):
        return pltpu.make_async_copy(src, dst, in_ss.at[i])

    def save(i, src, dst):
        return pltpu.make_async_copy(src, dst, out_ss.at[i])

    def save_tokens(c, m):
        return save(3 + 2 * m + jnp.where(c == core, 0, 1), tt_s.at[c, m], tt_hbm.at[c, m])

    loads = [load(0, x_hbm, x_ref)]
    for k in range(4):
        cols = pl.ds(k * width, width)
        loads.append(load(1 + k, win_hbm.at[:, cols], win_ref.at[:, cols]))
    loads.append(load(5, wout_hbm, wout_ref))
    loads.append(load(6, owner_hbm, owner_ref))
    loads.append(load(7, slot_hbm, slot_ref))
    for one in loads:
        one.start()

    @pl.when(sec == ns - 1)
    def _():
        load(8, og_hbm, g_s).start()

    barrier = pltpu.get_barrier_semaphore()
    peers = [other]
    peers += [(wrap(sec + d, ns), smp, core) for d in range(1, ns)]
    peers += [x_peer(d) for d in range(1, nx)]
    peers += [z_peer(d) for d in range(1, nz)]
    for peer in peers:
        pl.semaphore_signal(barrier, inc=1, device_id=peer, device_id_type=MESH)

    row_id = lax.broadcasted_iota(jnp.int32, (length, length), 0)
    col_id = lax.broadcasted_iota(jnp.int32, (length, length), 1)

    def forward():
        all_rows = micro * length
        loads[0].wait()
        xn, rx = normed(x_ref[...].reshape(all_rows, width).astype(F32))
        xn_s[...] = xn.reshape(xn_s.shape)
        rx_s[...] = rx.reshape(rx_s.shape)
        xb = xn.astype(BF)
        hx_s[1] = xb.reshape(micro, length, width)
        for k in range(4):
            loads[1 + k].wait()
            block = win_ref[:, k * width:(k + 1) * width]
            pre = mm(xb, block)
            s = sigmoid(pre)
            act = (pre * s).astype(BF)
            down = slope(pre, s)
            for m in range(micro):
                act_s[m, k] = act[m * length:(m + 1) * length]
                slope_s[m, k] = down[m * length:(m + 1) * length]
            wint_s[k] = block.T
        causal = row_id >= col_id
        for m in range(micro):
            vt_s[m] = act_s[m, 1].T
            mixed = []
            for h in range(HEADS):
                cols = slice(h * hs, (h + 1) * hs)
                z = mm_nt(act_s[m, 2, :, cols], act_s[m, 3, :, cols]) * scale
                s = sigmoid(z)
                wt = jnp.where(causal, z * s, 0.0).astype(BF)
                for r in range(2):
                    w_s[m, h, r] = wt[r * mid:(r + 1) * mid].T
                zs_s[m, h] = jnp.where(causal, slope(z, s), 0.0) * scale
                mixed.append(mm(wt, act_s[m, 1, :, cols]))
            mn, rm = normed(jnp.concatenate(mixed, -1))
            mn_s[m] = mn
            rm_s[m] = rm
            hx_s[0, m] = (mn * act_s[m, 0].astype(F32)).astype(BF)
        loads[5].wait()
        woutt_s[...] = wout_ref[...].T

    first = jnp.where(core == 0, 1, nx - 1)
    second = nx - first

    def flip(v, mask):
        pair = v + 1 - 2 * lax.rem(v, 2)
        return jnp.where(mask == 1, pair, nx - 1 - v)

    def x_at(x):
        return (sec, zz * nx + x, core)

    def g1_copy(k):
        return remote(
            gw_s.at[k, pl.ds(2, 2)], g1_r.at[k], g1_ss.at[k], g1_rs.at[k], x_at(flip(xx, first))
        )

    def g2_copy(k):
        return remote(g2_s.at[k], g2_r.at[k], g2_ss.at[k], g2_rs.at[k], x_at(flip(xx, second)))

    def gz_copy(k, d):
        return remote(
            gz_s.at[wrap(zz + d, nz), k], gz_r.at[d, k], gz_ss.at[d, k], gz_rs.at[d, k], z_peer(d)
        )

    def d_copy(k, m):
        return remote(d_s.at[1 - core, k, m], d_r.at[k, m], d_ss.at[k, m], d_rs.at[k, m], other)

    def gradient(k, kind):
        for m in range(micro):
            d_copy(k, m).wait_recv()
        part = mm(lt_s[kind, 0], d_s[core, k].reshape(micro * length, half))
        part = part + mm(lt_s[kind, 1], d_r[k].reshape(micro * length, half))
        part = part.astype(BF)
        for x in range(nx):
            slot = jnp.where(
                xx == x, 0, jnp.where(flip(xx, second) == x, 1, jnp.where(flip(xx, first) == x, 2, 3))
            )
            for z in range(nz):
                at = (z * nx + x) * rows
                gw_s[k, slot, z * rows:(z + 1) * rows, :] = part[at:at + rows]
        g1_copy(k).start()

    def keep(m, k, at, value):
        d_s[0, k, m, at] = value[:, :half]
        d_s[1, k, m, at] = value[:, half:]

    def backward(m, r, carried):
        at = slice(r * mid, (r + 1) * mid)
        g = g_s[m, at]
        keep(m, 0, at, g)
        if r == 0:
            d_copy(0, m).start()
        dh = mm(g, woutt_s[...])
        mn = mn_s[m, at]
        dpre = [(dh * mn * slope_s[m, 0, at]).astype(BF)]
        dmix = norm_back(dh * act_s[m, 0, at].astype(F32), mn, rm_s[m, at]).astype(BF)
        dv, dq, dk = [], [], []
        for h in range(HEADS):
            cols = slice(h * hs, (h + 1) * hs)
            dm = dmix[:, cols]
            dw = mm(dm, vt_s[m, cols])
            dv.append(mm(w_s[m, h, r], dm))
            dz = (dw * zs_s[m, h, at]).astype(BF)
            dq.append(mm(dz, act_s[m, 3, :, cols]))
            dk.append(mm(dz.T, act_s[m, 2, at, cols]))
        dv, dq, dk = (jnp.concatenate(part, -1) for part in (dv, dq, dk))
        if r == 1:
            carried = (dv[:mid], dk[:mid])
            dv, dk = dv[mid:], dk[mid:]
        else:
            dv, dk = dv[:mid] + carried[0], dk[:mid] + carried[1]
        for k, part in enumerate((dv, dq, dk)):
            dpre.append((part * slope_s[m, k + 1, at]).astype(BF))
        for k in range(4):
            keep(m, k + 1, at, dpre[k])
            if r == 0:
                d_copy(k + 1, m).start()
        dxn = mm(dpre[0], wint_s[0])
        for k in range(1, 4):
            dxn = dxn + mm(dpre[k], wint_s[k])
        below = norm_back(dxn, xn_s[m, at], rx_s[m, at]) + g.astype(F32)
        below_s[m, at] = below.astype(BF)
        return carried

    def pack_plan(m):
        owner = owner_ref[m:m + 1, :]
        spread = jnp.broadcast_to(owner.astype(F32), (length, length))
        same = (spread == spread.T) & (lax.div(row_id, BLOCK) == lax.div(col_id, BLOCK)) & (row_id < col_id)
        rank = jnp.sum(jnp.where(same, 1.0, 0.0), 0, keepdims=True).astype(jnp.int32)
        place = owner - sec * (nz * nx)
        mine = (place >= 0) & (place < nz * nx)
        place = jnp.where(mine, place, 0)
        block = lax.div(lax.broadcasted_iota(jnp.int32, (1, length), 1), BLOCK)
        to = (lax.rem(place, nx) * nz + lax.div(place, nx)) * piece + block * cap + rank
        to = jnp.where(mine, to, -1)
        plan = jnp.where(row_id == to, 1.0, 0.0).astype(BF)
        p_s[m] = plan
        name = slot_ref[m:m + 1, :] + 1
        high, low = lax.div(name, 32), lax.rem(name, 32)
        both = jnp.where(row_id < length // 2, high, low).astype(F32).astype(BF)
        return mm_nt(plan, both).astype(BF)

    def x_start(pack, inbox, ss, rs):
        inbox[0] = pack[xx]
        for d in range(1, nx):
            remote(pack.at[wrap(xx + d, nx)], inbox.at[d], ss.at[d], rs.at[d], x_peer(d)).start()

    def z_start(inbox, outbox, total, xs, xr, ss, rs):
        for d in range(1, nx):
            remote(inbox.at[d], inbox.at[d], xs.at[d], xr.at[d], x_peer(d)).wait_recv()
        src = lax.div(lax.rem(row_id, nx * piece), piece) * (nz * piece)
        src = src + lax.div(row_id, nx * piece) * piece + lax.rem(row_id, piece)
        turn = jnp.where(src == col_id, 1.0, 0.0).astype(BF)
        stacked = inbox[...].reshape(length, inbox.shape[-1])
        moved = mm(turn, stacked).astype(BF)
        outbox[...] = moved.reshape(outbox.shape)
        total[0] = outbox[zz]
        for d in range(1, nz):
            remote(outbox.at[wrap(zz + d, nz)], total.at[d], ss.at[d], rs.at[d], z_peer(d)).start()

    def core_start(mine, zs, zr, ss, rs):
        for d in range(1, nz):
            remote(mine.at[d], mine.at[d], zs.at[d], zr.at[d], z_peer(d)).wait_recv()
        remote(mine, mine, ss, rs, other).start()

    def prepare_own():
        ids = jnp.concatenate([pack_plan(m) for m in range(micro)], -1)
        idp_s[...] = ids.reshape(idp_s.shape)
        for kind in range(2):
            lt_s[kind, 0] = hx_s[kind].reshape(micro * length, width).T

    def prepare_sends():
        remote(hx_s, hx_o, hx_ss.at[0], hx_rs.at[0], other).start()
        x_start(idp_s, idx_r, ix_ss.at[0], ix_rs.at[0])

    def ids_along_z():
        z_start(idx_r, idz_s, idt_s.at[core], ix_ss.at[0], ix_rs.at[0], iz_ss.at[0], iz_rs.at[0])

    def prepare_other():
        remote(hx_s, hx_o, hx_ss.at[0], hx_rs.at[0], other).wait_recv()
        for kind in range(2):
            lt_s[kind, 1] = hx_o[kind].reshape(micro * length, width).T

    def ids_over():
        core_start(idt_s.at[core], iz_ss.at[0], iz_rs.at[0], ic_ss.at[0], ic_rs.at[0])

    def ids_done():
        remote(idt_s.at[1 - core], idt_s.at[1 - core], ic_ss.at[0], ic_rs.at[0], other).wait_recv()
        hits = jnp.zeros((own_rows, 1), F32)
        own_id = lax.broadcasted_iota(jnp.int32, (own_rows, length), 0).astype(F32)
        for c in range(2):
            for m in range(micro):
                both = idt_s[c, :, :, m * LANES:(m + 1) * LANES].reshape(length, LANES).astype(F32).T
                name = both[:1] * 32.0 + both[LANES // 2:LANES // 2 + 1] - 1.0
                hot = jnp.where(own_id == name, 1.0, 0.0)
                hits = hits + jnp.sum(hot, -1, keepdims=True)
                oh_s[:, (c * micro + m) * length:(c * micro + m + 1) * length] = hot.astype(BF)
        for b in range(own_rows // LANES):
            column = hits[b * LANES:(b + 1) * LANES]
            hits_ref[b:b + 1, :] = jnp.broadcast_to(column, (LANES, LANES)).T[:1]
        save(0, hits_ref, hits_hbm).start()
        save(2, oh_s, oh_hbm).start()

    forward()
    for one in loads[6:]:
        one.wait()

    @pl.when(sec == ns - 1)
    def _():
        load(8, og_hbm, g_s).wait()

    pl.semaphore_wait(barrier, len(peers))

    early = ns // 2

    @pl.when(sec < ns - 1)
    def _():
        prepare_own()
        prepare_sends()

    @pl.when(sec < early)
    def _():
        ids_along_z()
        prepare_other()
        ids_over()
        ids_done()

    def hop(m, r):
        at = pl.ds(r * mid, mid)
        return remote(
            below_s.at[m, at], g_s.at[m, at], hop_ss.at[m, r], hop_rs.at[m, r],
            (wrap(sec + ns - 1, ns), smp, core),
        )

    def token(m, r, to):
        at = pl.ds(r * mid, mid)
        return remote(
            below_s.at[m, at], tk_s.at[m, at], tk_ss.at[m, r, to], tk_rs.at[m, r], (to, smp, core)
        )

    far_first = sorted(range(1, ns), key=lambda to: -min(to, ns - to))

    def pack(m):
        packed = mm(p_s[m], tk_s[m]).astype(BF)
        tp_s[m] = packed.reshape(tp_s.shape[1:])
        x_start(tp_s.at[m], tx_r.at[m], ix_ss.at[1 + m], ix_rs.at[1 + m])

    @pl.loop(0, micro)
    def _(m):
        carried = None
        for r in (1, 0):
            @pl.when(sec < ns - 1)
            def _():
                hop(m, r).wait_recv()

            carried = backward(m, r, carried)

            @pl.when(sec > 0)
            def _():
                hop(m, r).start()

            @pl.when(sec == 0)
            def _():
                for to in far_first:
                    token(m, r, to).start()

        @pl.when(sec == 0)
        def _():
            tk_s[m] = below_s[m]
            pack(m)

    @pl.when(sec == ns - 1)
    def _():
        prepare_own()
        prepare_sends()

    @pl.when(sec >= early)
    def _():
        prepare_other()

    def get_tokens(m):
        for r in range(2):
            token(m, r, 1).wait_recv()
        pack(m)

    def by_section(places):
        at = jnp.int32(places[-1])
        for number in range(len(places) - 2, -1, -1):
            at = jnp.where(sec == number, places[number], at)
        return at

    def on_step(step, places, action):
        start = [by_section(place) for place in places]

        @pl.when((step == start[0]) | (step == start[1]))
        def _():
            action(jnp.where(step == start[1], 1, 0))

    def send_over(m):
        core_start(tt_s.at[core, m], iz_ss.at[1 + m], iz_rs.at[1 + m], ic_ss.at[1 + m], ic_rs.at[1 + m])
        save_tokens(core, m).start()

    @pl.loop(0, 10)
    def _(step):
        @pl.when(step < PARTS)
        def _():
            gradient(step, jnp.minimum(step, 1))

        @pl.when((step >= LAG) & (step < PARTS + LAG))
        def _():
            k = step - LAG
            g1_copy(k).wait_recv()
            total = gw_s[k, 1].astype(F32) + g1_r[k, 1].astype(F32)
            g2_s[k] = total.astype(BF)
            g2_copy(k).start()

        @pl.when((step > LAG) & (step <= PARTS + LAG))
        def _():
            k = step - LAG - 1
            g2_copy(k).wait_recv()
            total = gw_s[k, 0].astype(F32) + g1_r[k, 0].astype(F32) + g2_r[k].astype(F32)
            total = total.astype(BF)
            for z in range(nz):
                gz_s[z, k] = total[z * rows:(z + 1) * rows]
            for d in range(1, nz):
                gz_copy(k, d).start()

        for place, action in ((1, ids_along_z), (3, ids_over), (5, ids_done)):
            @pl.when((step == place) & (sec >= early))
            def _():
                action()

        on_step(step, ((-1, 4, 5, 6), (-1, 5, 6, 7)), get_tokens)
        on_step(
            step, ((2, 5, 6, 7), (4, 7, 7, 8)),
            lambda m: z_start(
                tx_r.at[m], tz_s.at[m], tt_s.at[core, m],
                ix_ss.at[1 + m], ix_rs.at[1 + m], iz_ss.at[1 + m], iz_rs.at[1 + m],
            ),
        )
        on_step(
            step, ((4, 7, 8, 8), (6, 8, 9, 9)),
            send_over,
        )

    total = gz_s[zz].astype(F32)
    for d in range(1, nz):
        for k in range(PARTS):
            gz_copy(k, d).wait_recv()
        total = total + gz_r[d].astype(F32)
    f_s[core] = total.astype(BF)
    remote(f_s.at[core], f_s.at[core], f_ss.at[0], f_rs.at[0], other).start()

    for m in range(micro):
        remote(
            tt_s.at[1 - core, m], tt_s.at[1 - core, m], ic_ss.at[1 + m], ic_rs.at[1 + m], other
        ).wait_recv()
        save_tokens(1 - core, m).start()
    remote(f_s.at[1 - core], f_s.at[1 - core], f_ss.at[0], f_rs.at[0], other).wait_recv()
    save(1, f_s, f_hbm).start()

    remote(hx_s, hx_o, hx_ss.at[0], hx_rs.at[0], other).wait_send()
    remote(f_s.at[core], f_s.at[core], f_ss.at[0], f_rs.at[0], other).wait_send()

    @pl.loop(0, PARTS)
    def _(k):
        for m in range(micro):
            d_copy(k, m).wait_send()
        g1_copy(k).wait_send()
        g2_copy(k).wait_send()
        for d in range(1, nz):
            gz_copy(k, d).wait_send()

    for i in range(1 + micro):
        pack_from = idp_s if i == 0 else tp_s.at[i - 1]
        inbox = idx_r if i == 0 else tx_r.at[i - 1]
        outbox = idz_s if i == 0 else tz_s.at[i - 1]
        full = idt_s.at[core] if i == 0 else tt_s.at[core, i - 1]
        for d in range(1, nx):
            remote(
                pack_from.at[wrap(xx + d, nx)], inbox.at[d], ix_ss.at[i, d], ix_rs.at[i, d], x_peer(d)
            ).wait_send()
        for d in range(1, nz):
            remote(
                outbox.at[wrap(zz + d, nz)], full.at[d], iz_ss.at[i, d], iz_rs.at[i, d], z_peer(d)
            ).wait_send()
        remote(full, full, ic_ss.at[i], ic_rs.at[i], other).wait_send()
    @pl.when(sec > 0)
    def _():
        for m in range(micro):
            for r in range(2):
                hop(m, r).wait_send()

    for m in range(micro):
        @pl.when(sec == 0)
        def _():
            for to in range(1, ns):
                for r in range(2):
                    token(m, r, to).wait_send()

    save(0, hits_ref, hits_hbm).wait()
    save(1, f_s, f_hbm).wait()
    save(2, oh_s, oh_hbm).wait()
    for m in range(micro):
        for c in (core, 1 - core):
            save_tokens(c, m).wait()


def finish(
    factor,
    oh_hbm, tt_hbm, hits_hbm, f_hbm, table_in, moment_in, second_in,
    gi_hbm, go_hbm, table_hbm, moment_hbm, second_hbm,
    oh_ref, tt_ref, hits_ref, f_ref, table_ref, moment_ref, second_ref, gi_s, go_s, table_s, moment_s, second_s, in_sems, sems,
):
    half = f_ref.shape[-1]
    width = 2 * half
    blocks = oh_ref.shape[0] // LANES

    copies = []

    loads = [
        pltpu.make_async_copy(src, dst, in_sems.at[i])
        for i, (src, dst) in enumerate(((tt_hbm, tt_ref), (hits_hbm, hits_ref), (second_in, second_ref), (f_hbm, f_ref)))
    ]

    def row_loads(b):
        at = pl.ds(b * LANES, LANES)
        pairs = ((oh_hbm, oh_ref), (moment_in, moment_ref), (table_in, table_ref))
        return [
            pltpu.make_async_copy(src.at[at], dst.at[at], in_sems.at[4 + 3 * b + i])
            for i, (src, dst) in enumerate(pairs)
        ]

    for load in loads[:3]:
        load.start()
    for b in range(blocks):
        for load in row_loads(b):
            load.start()
    loads[3].start()
    for load in loads[:3]:
        load.wait()
    tokens = tt_ref[...].reshape(oh_ref.shape[1], width)

    def put(src, dst):
        copy = pltpu.make_async_copy(src, dst, sems.at[len(copies)])
        copy.start()
        copies.append(copy)

    for b in range(blocks):
        at = pl.ds(b * LANES, LANES)
        for load in row_loads(b):
            load.wait()
        grad = mm(oh_ref[at, :], tokens)
        hit = jnp.broadcast_to(hits_ref[b:b + 1, :], (LANES, LANES)).T > 0.5
        wide = jnp.concatenate([hit] * (width // LANES), -1)
        square = jnp.mean(grad * grad, -1, keepdims=True)
        square = jnp.broadcast_to(square, (LANES, LANES))
        old = jnp.broadcast_to(second_ref[b:b + 1, :], (LANES, LANES)).T
        new = jnp.where(hit, BETA_TWO * old + (1.0 - BETA_TWO) * square, old)
        second_s[b:b + 1, :] = new.T[:1]
        old_moment = moment_ref[at, :]
        moment = jnp.where(wide, BETA_ONE * old_moment + (1.0 - BETA_ONE) * grad, old_moment)
        moment_s[at, :] = moment
        put(moment_s.at[at], moment_hbm.at[at])
        old_table = table_ref[at, :]
        below = jnp.concatenate([jnp.sqrt(new) + ADAM_EPS] * (width // LANES), -1)
        table_s[at, :] = jnp.where(wide, old_table - STEP_SIZE * moment / below, old_table)
        put(table_s.at[at], table_hbm.at[at])
    put(second_s, second_hbm)
    loads[3].wait()
    for c in range(2):
        go_s[:, c * half:(c + 1) * half] = f_ref[c, 0].astype(F32) * factor
        for k in range(4):
            at = k * width + c * half
            gi_s[:, at:at + half] = f_ref[c, k + 1].astype(F32) * factor
    put(go_s, go_hbm)
    put(gi_s, gi_hbm)
    for copy in copies:
        copy.wait()


def exchange(dims, x, og, w_in, w_out, owner, slot, own_rows):
    ns, nz, nx, cap = dims
    micro, length, width = x.shape
    half = width // 2
    rows = width // (nz * nx)
    dma = pltpu.SemaphoreType.DMA
    vm = pltpu.VMEM
    lx, lz = length // nx, length // nz
    streams = 1 + micro
    wide = LANES * micro
    scratch = [
        vm((own_rows // LANES, LANES), F32),
        vm((micro, length, width), BF),
        vm((width, 4 * width), BF),
        vm((width, width), BF),
        vm((micro, length), jnp.int32),
        vm((micro, length), jnp.int32),
        vm((4, width, width), BF),
        vm((width, width), BF),
        vm((micro, width, length), BF),
        vm((micro, length, width), F32),
        vm((micro, length, 1), F32),
        vm((micro, 4, length, width), BF),
        vm((micro, 4, length, width), F32),
        vm((micro, HEADS, 2, length, length // 2), BF),
        vm((micro, HEADS, length, length), F32),
        vm((micro, length, width), F32),
        vm((micro, length, 1), F32),
        vm((2, micro, length, width), BF),
        vm((2, micro, length, width), BF),
        vm((2, 2, width, micro * length), BF),
        vm((micro, length, width), BF),
        vm((micro, length, width), BF),
        vm((2, PARTS, micro, length, half), BF),
        vm((PARTS, micro, length, half), BF),
        vm((PARTS, nx, nz * rows, half), BF),
        vm((PARTS, 2, nz * rows, half), BF),
        vm((PARTS, nz * rows, half), BF),
        vm((PARTS, nz * rows, half), BF),
        vm((nz, PARTS, rows, half), BF),
        vm((nz, PARTS, rows, half), BF),
        vm((2, PARTS, rows, half), BF),
        vm((micro, length, length), BF),
        vm((micro, length, width), BF),
        vm((nx, lx, wide), BF),
        vm((nx, lx, wide), BF),
        vm((nz, lz, wide), BF),
        vm((2, nz, lz, wide), BF),
        vm((micro, nx, lx, width), BF),
        vm((micro, nx, lx, width), BF),
        vm((micro, nz, lz, width), BF),
        vm((2, micro, nz, lz, width), BF),
        vm((own_rows, 2 * micro * length), BF),
        dma((9,)), dma((3 + 2 * micro,)), dma((micro, 2)), dma((micro, 2)), dma((1,)), dma((1,)),
        dma((PARTS, micro)), dma((PARTS, micro)),
        dma((PARTS,)), dma((PARTS,)), dma((PARTS,)), dma((PARTS,)),
        dma((nz, PARTS)), dma((nz, PARTS)), dma((1,)), dma((1,)),
        dma((micro, 2, 4)), dma((micro, 2)),
        dma((streams, nx)), dma((streams, nx)),
        dma((streams, nz)), dma((streams, nz)),
        dma((streams,)), dma((streams,)),
    ]
    return pl.pallas_call(
        functools.partial(kernel, dims),
        out_shape=(
            jax.ShapeDtypeStruct((own_rows, 2 * micro * length), BF),
            jax.ShapeDtypeStruct((2, micro, nz, lz, width), BF),
            jax.ShapeDtypeStruct((own_rows // LANES, LANES), F32),
            jax.ShapeDtypeStruct((2, PARTS, rows, half), BF),
        ),
        in_specs=[pl.BlockSpec(memory_space=pltpu.HBM)] * 6,
        out_specs=[pl.BlockSpec(memory_space=pltpu.HBM)] * 4,
        scratch_shapes=scratch,
        compiler_params=pltpu.CompilerParams(
            collective_id=0, has_side_effects=True, vmem_limit_bytes=56 << 20
        ),
    )(x, og, w_in, w_out, owner, slot)


def local(nz, nx, saved_input, out_grad, w_in, w_out, item_owner, item_slot, table, moment, second):
    ns = lax.axis_size("section")
    micro, length, width = out_grad.shape[0], out_grad.shape[2], out_grad.shape[3]
    owners = ns * nz * nx
    cap = max(2, 2 * BLOCK // owners)
    own_rows = table.shape[0]
    rows = width // (nz * nx)
    hot, tokens_in, hits, grads = exchange(
        (ns, nz, nx, cap),
        saved_input[0, :, 0],
        out_grad[:, 0],
        w_in[0],
        w_out[0],
        item_owner.reshape(micro, length),
        item_slot.reshape(micro, length),
        own_rows,
    )
    tokens = micro * length * nz * nx * lax.axis_size("replica")
    lines = (own_rows // LANES, LANES)
    shapes = [(rows, 4 * width), (rows, width), (own_rows, width), (own_rows, width), lines]
    grad_in, grad_out, table_new, moment_new, second_new = pl.pallas_call(
        functools.partial(finish, float(tokens) ** (-0.5)),
        out_shape=[jax.ShapeDtypeStruct(shape, F32) for shape in shapes],
        in_specs=[pl.BlockSpec(memory_space=pltpu.HBM)] * 7,
        out_specs=[pl.BlockSpec(memory_space=pltpu.HBM)] * 5,
        scratch_shapes=[pltpu.VMEM(part.shape, part.dtype) for part in (hot, tokens_in, hits, grads)]
        + [pltpu.VMEM(shape, F32) for shape in shapes[2:]]
        + [pltpu.VMEM(shape, F32) for shape in shapes]
        + [pltpu.SemaphoreType.DMA((4 + 3 * lines[0],)), pltpu.SemaphoreType.DMA((2 * lines[0] + 3,))],
        compiler_params=pltpu.CompilerParams(vmem_limit_bytes=56 << 20),
    )(hot, tokens_in, hits, grads, table, moment, second.reshape(lines))
    return (grad_in[None], grad_out[None], table_new, moment_new, second_new.reshape(own_rows))


def solution(mesh):
    nx = 4
    nz = mesh.shape["sample"] // nx
    placed = (
        P("section", None, ("sample", "replica"), None, None),
        P(None, ("sample", "replica"), None, None),
        P("section", None, None),
        P("section", None, None),
        P(("sample", "replica"), None, None, None),
        P(("sample", "replica"), None, None),
        P(("section", "sample"), None),
        P(("section", "sample"), None),
        P(("section", "sample")),
    )
    return jax.shard_map(
        functools.partial(local, nz, nx),
        mesh=mesh,
        in_specs=placed,
        out_specs=(
            P("section", "sample", None),
            P("section", "sample", None),
            P(("section", "sample"), None),
            P(("section", "sample"), None),
            P(("section", "sample")),
        ),
        check_vma=False,
    )
```

```python
import functools

import jax
import jax.numpy as jnp
from jax import lax
from jax.experimental import pallas as pl
from jax.experimental.pallas import tpu as pltpu
from jax.sharding import PartitionSpec as P

HEADS = 4
BLOCK = 64
LN_EPS = 1e-05
BETA_ONE = 0.8
BETA_TWO = 0.9
STEP_SIZE = 0.05
ADAM_EPS = 1e-08

F32 = jnp.float32
BF = jnp.bfloat16
MESH = pl.DeviceIdType.MESH
PARTS = 5
LANES = 128
LAG = 2


def mm(a, b):
    return jnp.dot(a, b, preferred_element_type=F32)


def mm_nt(a, b):
    return lax.dot_general(a, b, (((1,), (1,)), ((), ())), preferred_element_type=F32)


def sigmoid(v):
    return 0.5 + 0.5 * jnp.tanh(0.5 * v)


def mean(v):
    return jnp.mean(v, -1, keepdims=True)


def normed(v):
    center = v - mean(v)
    inverse = lax.rsqrt(mean(center * center) + LN_EPS)
    return center * inverse, inverse


def norm_back(grad, norm, inverse):
    return inverse * (grad - mean(grad) - norm * mean(grad * norm))


def slope(v, s):
    return s * (1.0 + v * (1.0 - s))


def kernel(
    dims,
    x_hbm, og_hbm, win_hbm, wout_hbm, owner_hbm, slot_hbm,
    oh_hbm, tt_hbm, hits_hbm, f_hbm,
    hits_ref, x_ref, win_ref, wout_ref, owner_ref, slot_ref,
    wint_s, woutt_s, vt_s, xn_s, rx_s, act_s, slope_s, w_s, zs_s, mn_s, rm_s,
    hx_s, hx_o, lt_s, g_s, below_s, d_s, d_r,
    gw_s, g1_r, g2_s, g2_r, gz_s, gz_r, f_s,
    p_s, tk_s, idp_s, idx_r, idz_s, idt_s, tp_s, tx_r, tz_s, tt_s, oh_s,
    in_ss, out_ss, hop_ss, hop_rs, hx_ss, hx_rs, d_ss, d_rs,
    g1_ss, g1_rs, g2_ss, g2_rs, gz_ss, gz_rs, f_ss, f_rs,
    tk_ss, tk_rs, ix_ss, ix_rs, iz_ss, iz_rs, ic_ss, ic_rs,
):
    ns, nz, nx, cap = dims
    micro, length, width = x_ref.shape
    half = width // 2
    mid = length // 2
    hs = width // HEADS
    scale = hs ** (-0.5)
    rows = width // (nz * nx)
    own_rows = oh_hbm.shape[0]
    piece = length // (nz * nx)
    sec = lax.axis_index("section")
    smp = lax.axis_index("sample")
    core = lax.axis_index("replica")
    zz, xx = lax.div(smp, nx), lax.rem(smp, nx)

    def wrap(v, n):
        return lax.rem(v, n)

    def x_peer(d):
        return (sec, zz * nx + wrap(xx + d, nx), core)

    z_order = sorted(range(1, nz), key=lambda d: -min(d, nz - d))

    def z_peer(d):
        return (sec, wrap(zz + d, nz) * nx + xx, core)

    other = (sec, smp, 1 - core)

    def remote(src, dst, ss, rs, dev):
        return pltpu.make_async_remote_copy(
            src_ref=src, dst_ref=dst, send_sem=ss, recv_sem=rs, device_id=dev, device_id_type=MESH
        )

    def load(i, src, dst):
        return pltpu.make_async_copy(src, dst, in_ss.at[i])

    def save(i, src, dst):
        return pltpu.make_async_copy(src, dst, out_ss.at[i])

    def save_tokens(c, m):
        return save(3 + 2 * m + jnp.where(c == core, 0, 1), tt_s.at[c, m], tt_hbm.at[c, m])

    loads = [load(0, x_hbm, x_ref)]
    for k in range(4):
        cols = pl.ds(k * width, width)
        loads.append(load(1 + k, win_hbm.at[:, cols], win_ref.at[:, cols]))
    loads.append(load(5, wout_hbm, wout_ref))
    loads.append(load(6, owner_hbm, owner_ref))
    loads.append(load(7, slot_hbm, slot_ref))
    for one in loads:
        one.start()

    @pl.when(sec == ns - 1)
    def _():
        load(8, og_hbm, g_s).start()

    barrier = pltpu.get_barrier_semaphore()
    peers = [other]
    peers += [(wrap(sec + d, ns), smp, core) for d in range(1, ns)]
    peers += [x_peer(d) for d in range(1, nx)]
    peers += [z_peer(d) for d in range(1, nz)]
    for peer in peers:
        pl.semaphore_signal(barrier, inc=1, device_id=peer, device_id_type=MESH)

    row_id = lax.broadcasted_iota(jnp.int32, (length, length), 0)
    col_id = lax.broadcasted_iota(jnp.int32, (length, length), 1)

    def forward():
        all_rows = micro * length
        loads[0].wait()
        xn, rx = normed(x_ref[...].reshape(all_rows, width).astype(F32))
        xn_s[...] = xn.reshape(xn_s.shape)
        rx_s[...] = rx.reshape(rx_s.shape)
        xb = xn.astype(BF)
        hx_s[1] = xb.reshape(micro, length, width)
        for k in range(4):
            loads[1 + k].wait()
            block = win_ref[:, k * width:(k + 1) * width]
            pre = mm(xb, block)
            s = sigmoid(pre)
            act = (pre * s).astype(BF)
            down = slope(pre, s)
            for m in range(micro):
                act_s[m, k] = act[m * length:(m + 1) * length]
                slope_s[m, k] = down[m * length:(m + 1) * length]
            wint_s[k] = block.T
        causal = row_id >= col_id
        for m in range(micro):
            vt_s[m] = act_s[m, 1].T
            mixed = []
            for h in range(HEADS):
                cols = slice(h * hs, (h + 1) * hs)
                z = mm_nt(act_s[m, 2, :, cols], act_s[m, 3, :, cols]) * scale
                s = sigmoid(z)
                wt = jnp.where(causal, z * s, 0.0).astype(BF)
                for r in range(2):
                    w_s[m, h, r] = wt[r * mid:(r + 1) * mid].T
                zs_s[m, h] = jnp.where(causal, slope(z, s), 0.0) * scale
                mixed.append(mm(wt, act_s[m, 1, :, cols]))
            mn, rm = normed(jnp.concatenate(mixed, -1))
            mn_s[m] = mn
            rm_s[m] = rm
            hx_s[0, m] = (mn * act_s[m, 0].astype(F32)).astype(BF)
        loads[5].wait()
        woutt_s[...] = wout_ref[...].T

    first = jnp.where(core == 0, 1, nx - 1)
    second = nx - first

    def flip(v, mask):
        pair = v + 1 - 2 * lax.rem(v, 2)
        return jnp.where(mask == 1, pair, nx - 1 - v)

    def x_at(x):
        return (sec, zz * nx + x, core)

    def g1_copy(k):
        return remote(
            gw_s.at[k, pl.ds(2, 2)], g1_r.at[k], g1_ss.at[k], g1_rs.at[k], x_at(flip(xx, first))
        )

    def g2_copy(k):
        return remote(g2_s.at[k], g2_r.at[k], g2_ss.at[k], g2_rs.at[k], x_at(flip(xx, second)))

    def gz_copy(k, d):
        return remote(
            gz_s.at[wrap(zz + d, nz), k], gz_r.at[d, k], gz_ss.at[d, k], gz_rs.at[d, k], z_peer(d)
        )

    def d_copy(k, m):
        return remote(d_s.at[1 - core, k, m], d_r.at[k, m], d_ss.at[k, m], d_rs.at[k, m], other)

    def gradient(k, kind):
        for m in range(micro):
            d_copy(k, m).wait_recv()
        part = mm(lt_s[kind, 0], d_s[core, k].reshape(micro * length, half))
        part = part + mm(lt_s[kind, 1], d_r[k].reshape(micro * length, half))
        part = part.astype(BF)
        for x in range(nx):
            slot = jnp.where(
                xx == x, 0, jnp.where(flip(xx, second) == x, 1, jnp.where(flip(xx, first) == x, 2, 3))
            )
            for z in range(nz):
                at = (z * nx + x) * rows
                gw_s[k, slot, z * rows:(z + 1) * rows, :] = part[at:at + rows]
        g1_copy(k).start()

    def keep(m, k, at, value):
        d_s[0, k, m, at] = value[:, :half]
        d_s[1, k, m, at] = value[:, half:]

    def backward(m, r, carried):
        at = slice(r * mid, (r + 1) * mid)
        g = g_s[m, at]
        keep(m, 0, at, g)
        if r == 0:
            d_copy(0, m).start()
        dh = mm(g, woutt_s[...])
        mn = mn_s[m, at]
        dpre = [(dh * mn * slope_s[m, 0, at]).astype(BF)]
        dmix = norm_back(dh * act_s[m, 0, at].astype(F32), mn, rm_s[m, at]).astype(BF)
        dv, dq, dk = [], [], []
        for h in range(HEADS):
            cols = slice(h * hs, (h + 1) * hs)
            dm = dmix[:, cols]
            dw = mm(dm, vt_s[m, cols])
            dv.append(mm(w_s[m, h, r], dm))
            dz = (dw * zs_s[m, h, at]).astype(BF)
            dq.append(mm(dz, act_s[m, 3, :, cols]))
            dk.append(mm(dz.T, act_s[m, 2, at, cols]))
        dv, dq, dk = (jnp.concatenate(part, -1) for part in (dv, dq, dk))
        if r == 1:
            carried = (dv[:mid], dk[:mid])
            dv, dk = dv[mid:], dk[mid:]
        else:
            dv, dk = dv[:mid] + carried[0], dk[:mid] + carried[1]
        for k, part in enumerate((dv, dq, dk)):
            dpre.append((part * slope_s[m, k + 1, at]).astype(BF))
        for k in range(4):
            keep(m, k + 1, at, dpre[k])
            if r == 0:
                d_copy(k + 1, m).start()
        dxn = mm(dpre[0], wint_s[0])
        for k in range(1, 4):
            dxn = dxn + mm(dpre[k], wint_s[k])
        below = norm_back(dxn, xn_s[m, at], rx_s[m, at]) + g.astype(F32)
        below_s[m, at] = below.astype(BF)
        return carried

    def pack_plan(m):
        owner = owner_ref[m:m + 1, :]
        spread = jnp.broadcast_to(owner.astype(F32), (length, length))
        same = (spread == spread.T) & (lax.div(row_id, BLOCK) == lax.div(col_id, BLOCK)) & (row_id < col_id)
        rank = jnp.sum(jnp.where(same, 1.0, 0.0), 0, keepdims=True).astype(jnp.int32)
        place = owner - sec * (nz * nx)
        mine = (place >= 0) & (place < nz * nx)
        place = jnp.where(mine, place, 0)
        block = lax.div(lax.broadcasted_iota(jnp.int32, (1, length), 1), BLOCK)
        to = (lax.rem(place, nx) * nz + lax.div(place, nx)) * piece + block * cap + rank
        to = jnp.where(mine, to, -1)
        plan = jnp.where(row_id == to, 1.0, 0.0).astype(BF)
        p_s[m] = plan
        name = slot_ref[m:m + 1, :] + 1
        high, low = lax.div(name, 32), lax.rem(name, 32)
        both = jnp.where(row_id < length // 2, high, low).astype(F32).astype(BF)
        return mm_nt(plan, both).astype(BF)

    def x_start(pack, inbox, ss, rs):
        inbox[0] = pack[xx]
        for d in range(1, nx):
            remote(pack.at[wrap(xx + d, nx)], inbox.at[d], ss.at[d], rs.at[d], x_peer(d)).start()

    def z_start(inbox, outbox, total, xs, xr, ss, rs):
        for d in range(1, nx):
            remote(inbox.at[d], inbox.at[d], xs.at[d], xr.at[d], x_peer(d)).wait_recv()
        src = lax.div(lax.rem(row_id, nx * piece), piece) * (nz * piece)
        src = src + lax.div(row_id, nx * piece) * piece + lax.rem(row_id, piece)
        turn = jnp.where(src == col_id, 1.0, 0.0).astype(BF)
        stacked = inbox[...].reshape(length, inbox.shape[-1])
        moved = mm(turn, stacked).astype(BF)
        outbox[...] = moved.reshape(outbox.shape)
        total[0] = outbox[zz]
        for d in z_order:
            remote(outbox.at[wrap(zz + d, nz)], total.at[d], ss.at[d], rs.at[d], z_peer(d)).start()

    def core_start(mine, zs, zr, ss, rs):
        for d in range(1, nz):
            remote(mine.at[d], mine.at[d], zs.at[d], zr.at[d], z_peer(d)).wait_recv()
        remote(mine, mine, ss, rs, other).start()

    def prepare_own():
        ids = jnp.concatenate([pack_plan(m) for m in range(micro)], -1)
        idp_s[...] = ids.reshape(idp_s.shape)
        for kind in range(2):
            lt_s[kind, 0] = hx_s[kind].reshape(micro * length, width).T

    def prepare_sends():
        remote(hx_s, hx_o, hx_ss.at[0], hx_rs.at[0], other).start()
        x_start(idp_s, idx_r, ix_ss.at[0], ix_rs.at[0])

    def ids_along_z():
        z_start(idx_r, idz_s, idt_s.at[core], ix_ss.at[0], ix_rs.at[0], iz_ss.at[0], iz_rs.at[0])

    def prepare_other():
        remote(hx_s, hx_o, hx_ss.at[0], hx_rs.at[0], other).wait_recv()
        for kind in range(2):
            lt_s[kind, 1] = hx_o[kind].reshape(micro * length, width).T

    def ids_over():
        core_start(idt_s.at[core], iz_ss.at[0], iz_rs.at[0], ic_ss.at[0], ic_rs.at[0])

    def ids_done():
        remote(idt_s.at[1 - core], idt_s.at[1 - core], ic_ss.at[0], ic_rs.at[0], other).wait_recv()
        hits = jnp.zeros((own_rows, 1), F32)
        own_id = lax.broadcasted_iota(jnp.int32, (own_rows, length), 0).astype(F32)
        for c in range(2):
            for m in range(micro):
                both = idt_s[c, :, :, m * LANES:(m + 1) * LANES].reshape(length, LANES).astype(F32).T
                name = both[:1] * 32.0 + both[LANES // 2:LANES // 2 + 1] - 1.0
                hot = jnp.where(own_id == name, 1.0, 0.0)
                hits = hits + jnp.sum(hot, -1, keepdims=True)
                oh_s[:, (c * micro + m) * length:(c * micro + m + 1) * length] = hot.astype(BF)
        for b in range(own_rows // LANES):
            column = hits[b * LANES:(b + 1) * LANES]
            hits_ref[b:b + 1, :] = jnp.broadcast_to(column, (LANES, LANES)).T[:1]
        save(0, hits_ref, hits_hbm).start()
        save(2, oh_s, oh_hbm).start()

    forward()
    for one in loads[6:]:
        one.wait()

    @pl.when(sec == ns - 1)
    def _():
        load(8, og_hbm, g_s).wait()

    pl.semaphore_wait(barrier, len(peers))

    early = ns // 2

    @pl.when(sec < ns - 1)
    def _():
        prepare_own()
        prepare_sends()

    @pl.when(sec < early)
    def _():
        ids_along_z()
        prepare_other()
        ids_over()
        ids_done()

    def hop(m, r):
        at = pl.ds(r * mid, mid)
        return remote(
            below_s.at[m, at], g_s.at[m, at], hop_ss.at[m, r], hop_rs.at[m, r],
            (wrap(sec + ns - 1, ns), smp, core),
        )

    def token(m, r, to):
        at = pl.ds(r * mid, mid)
        return remote(
            below_s.at[m, at], tk_s.at[m, at], tk_ss.at[m, r, to], tk_rs.at[m, r], (to, smp, core)
        )

    far_first = sorted(range(1, ns), key=lambda to: -min(to, ns - to))

    def pack(m):
        packed = mm(p_s[m], tk_s[m]).astype(BF)
        tp_s[m] = packed.reshape(tp_s.shape[1:])
        x_start(tp_s.at[m], tx_r.at[m], ix_ss.at[1 + m], ix_rs.at[1 + m])

    @pl.loop(0, micro)
    def _(m):
        carried = None
        for r in (1, 0):
            @pl.when(sec < ns - 1)
            def _():
                hop(m, r).wait_recv()

            carried = backward(m, r, carried)

            @pl.when(sec > 0)
            def _():
                hop(m, r).start()

            @pl.when(sec == 0)
            def _():
                for to in far_first:
                    token(m, r, to).start()

        @pl.when(sec == 0)
        def _():
            tk_s[m] = below_s[m]

            @pl.when(m < micro - 1)
            def _():
                pack(m)

    @pl.when(sec == ns - 1)
    def _():
        prepare_own()
        prepare_sends()

    @pl.when(sec >= early)
    def _():
        prepare_other()

    def get_tokens(m):
        @pl.when(sec > 0)
        def _():
            for r in range(2):
                token(m, r, 1).wait_recv()

        pack(m)

    def by_section(places):
        at = jnp.int32(places[-1])
        for number in range(len(places) - 2, -1, -1):
            at = jnp.where(sec == number, places[number], at)
        return at

    def on_step(step, places, action):
        start = [by_section(place) for place in places]

        @pl.when((step == start[0]) | (step == start[1]))
        def _():
            action(jnp.where(step == start[1], 1, 0))

    def send_over(m):
        core_start(tt_s.at[core, m], iz_ss.at[1 + m], iz_rs.at[1 + m], ic_ss.at[1 + m], ic_rs.at[1 + m])
        save_tokens(core, m).start()

    @pl.loop(0, 10)
    def _(step):
        @pl.when(step < PARTS)
        def _():
            gradient(step, jnp.minimum(step, 1))

        @pl.when((step >= LAG) & (step < PARTS + LAG))
        def _():
            k = step - LAG
            g1_copy(k).wait_recv()
            total = gw_s[k, 1].astype(F32) + g1_r[k, 1].astype(F32)
            g2_s[k] = total.astype(BF)
            g2_copy(k).start()

        @pl.when((step > LAG) & (step <= PARTS + LAG))
        def _():
            k = step - LAG - 1
            g2_copy(k).wait_recv()
            total = gw_s[k, 0].astype(F32) + g1_r[k, 0].astype(F32) + g2_r[k].astype(F32)
            total = total.astype(BF)
            for z in range(nz):
                gz_s[z, k] = total[z * rows:(z + 1) * rows]
            for d in z_order:
                gz_copy(k, d).start()

        for place, action in ((1, ids_along_z), (3, ids_over), (5, ids_done)):
            @pl.when((step == place) & (sec >= early))
            def _():
                action()

        on_step(step, ((-1, 4, 5, 6), (1, 5, 6, 7)), get_tokens)
        on_step(
            step, ((2, 5, 6, 7), (4, 7, 7, 8)),
            lambda m: z_start(
                tx_r.at[m], tz_s.at[m], tt_s.at[core, m],
                ix_ss.at[1 + m], ix_rs.at[1 + m], iz_ss.at[1 + m], iz_rs.at[1 + m],
            ),
        )
        on_step(
            step, ((6, 7, 8, 8), (8, 8, 9, 9)),
            send_over,
        )

    total = gz_s[zz].astype(F32)
    for d in range(1, nz):
        for k in range(PARTS):
            gz_copy(k, d).wait_recv()
        total = total + gz_r[d].astype(F32)
    f_s[core] = total.astype(BF)
    remote(f_s.at[core], f_s.at[core], f_ss.at[0], f_rs.at[0], other).start()

    for m in range(micro):
        remote(
            tt_s.at[1 - core, m], tt_s.at[1 - core, m], ic_ss.at[1 + m], ic_rs.at[1 + m], other
        ).wait_recv()
        save_tokens(1 - core, m).start()
    remote(f_s.at[1 - core], f_s.at[1 - core], f_ss.at[0], f_rs.at[0], other).wait_recv()
    save(1, f_s, f_hbm).start()

    remote(hx_s, hx_o, hx_ss.at[0], hx_rs.at[0], other).wait_send()
    remote(f_s.at[core], f_s.at[core], f_ss.at[0], f_rs.at[0], other).wait_send()

    @pl.loop(0, PARTS)
    def _(k):
        for m in range(micro):
            d_copy(k, m).wait_send()
        g1_copy(k).wait_send()
        g2_copy(k).wait_send()
        for d in range(1, nz):
            gz_copy(k, d).wait_send()

    for i in range(1 + micro):
        pack_from = idp_s if i == 0 else tp_s.at[i - 1]
        inbox = idx_r if i == 0 else tx_r.at[i - 1]
        outbox = idz_s if i == 0 else tz_s.at[i - 1]
        full = idt_s.at[core] if i == 0 else tt_s.at[core, i - 1]
        for d in range(1, nx):
            remote(
                pack_from.at[wrap(xx + d, nx)], inbox.at[d], ix_ss.at[i, d], ix_rs.at[i, d], x_peer(d)
            ).wait_send()
        for d in range(1, nz):
            remote(
                outbox.at[wrap(zz + d, nz)], full.at[d], iz_ss.at[i, d], iz_rs.at[i, d], z_peer(d)
            ).wait_send()
        remote(full, full, ic_ss.at[i], ic_rs.at[i], other).wait_send()
    @pl.when(sec > 0)
    def _():
        for m in range(micro):
            for r in range(2):
                hop(m, r).wait_send()

    for m in range(micro):
        @pl.when(sec == 0)
        def _():
            for to in range(1, ns):
                for r in range(2):
                    token(m, r, to).wait_send()

    save(0, hits_ref, hits_hbm).wait()
    save(1, f_s, f_hbm).wait()
    save(2, oh_s, oh_hbm).wait()
    for m in range(micro):
        for c in (core, 1 - core):
            save_tokens(c, m).wait()


def finish(
    factor,
    oh_hbm, tt_hbm, hits_hbm, f_hbm, table_in, moment_in, second_in,
    gi_hbm, go_hbm, table_hbm, moment_hbm, second_hbm,
    oh_ref, tt_ref, hits_ref, f_ref, table_ref, moment_ref, second_ref, gi_s, go_s, table_s, moment_s, second_s, in_sems, sems,
):
    half = f_ref.shape[-1]
    width = 2 * half
    blocks = oh_ref.shape[0] // LANES

    copies = []

    loads = [
        pltpu.make_async_copy(src, dst, in_sems.at[i])
        for i, (src, dst) in enumerate(((tt_hbm, tt_ref), (hits_hbm, hits_ref), (second_in, second_ref), (f_hbm, f_ref)))
    ]

    def row_loads(b):
        at = pl.ds(b * LANES, LANES)
        pairs = ((oh_hbm, oh_ref), (moment_in, moment_ref), (table_in, table_ref))
        return [
            pltpu.make_async_copy(src.at[at], dst.at[at], in_sems.at[4 + 3 * b + i])
            for i, (src, dst) in enumerate(pairs)
        ]

    for load in loads[:3]:
        load.start()
    for b in range(blocks):
        for load in row_loads(b):
            load.start()
    loads[3].start()
    for load in loads[:3]:
        load.wait()
    tokens = tt_ref[...].reshape(oh_ref.shape[1], width)

    def put(src, dst):
        copy = pltpu.make_async_copy(src, dst, sems.at[len(copies)])
        copy.start()
        copies.append(copy)

    for b in range(blocks):
        at = pl.ds(b * LANES, LANES)
        for load in row_loads(b):
            load.wait()
        grad = mm(oh_ref[at, :], tokens)
        hit = jnp.broadcast_to(hits_ref[b:b + 1, :], (LANES, LANES)).T > 0.5
        wide = jnp.concatenate([hit] * (width // LANES), -1)
        square = jnp.mean(grad * grad, -1, keepdims=True)
        square = jnp.broadcast_to(square, (LANES, LANES))
        old = jnp.broadcast_to(second_ref[b:b + 1, :], (LANES, LANES)).T
        new = jnp.where(hit, BETA_TWO * old + (1.0 - BETA_TWO) * square, old)
        second_s[b:b + 1, :] = new.T[:1]
        old_moment = moment_ref[at, :]
        moment = jnp.where(wide, BETA_ONE * old_moment + (1.0 - BETA_ONE) * grad, old_moment)
        moment_s[at, :] = moment
        put(moment_s.at[at], moment_hbm.at[at])
        old_table = table_ref[at, :]
        below = jnp.concatenate([jnp.sqrt(new) + ADAM_EPS] * (width // LANES), -1)
        table_s[at, :] = jnp.where(wide, old_table - STEP_SIZE * moment / below, old_table)
        put(table_s.at[at], table_hbm.at[at])
    put(second_s, second_hbm)
    loads[3].wait()
    for c in range(2):
        go_s[:, c * half:(c + 1) * half] = f_ref[c, 0].astype(F32) * factor
        for k in range(4):
            at = k * width + c * half
            gi_s[:, at:at + half] = f_ref[c, k + 1].astype(F32) * factor
    put(go_s, go_hbm)
    put(gi_s, gi_hbm)
    for copy in copies:
        copy.wait()


def exchange(dims, x, og, w_in, w_out, owner, slot, own_rows):
    ns, nz, nx, cap = dims
    micro, length, width = x.shape
    half = width // 2
    rows = width // (nz * nx)
    dma = pltpu.SemaphoreType.DMA
    vm = pltpu.VMEM
    lx, lz = length // nx, length // nz
    streams = 1 + micro
    wide = LANES * micro
    scratch = [
        vm((own_rows // LANES, LANES), F32),
        vm((micro, length, width), BF),
        vm((width, 4 * width), BF),
        vm((width, width), BF),
        vm((micro, length), jnp.int32),
        vm((micro, length), jnp.int32),
        vm((4, width, width), BF),
        vm((width, width), BF),
        vm((micro, width, length), BF),
        vm((micro, length, width), F32),
        vm((micro, length, 1), F32),
        vm((micro, 4, length, width), BF),
        vm((micro, 4, length, width), F32),
        vm((micro, HEADS, 2, length, length // 2), BF),
        vm((micro, HEADS, length, length), F32),
        vm((micro, length, width), F32),
        vm((micro, length, 1), F32),
        vm((2, micro, length, width), BF),
        vm((2, micro, length, width), BF),
        vm((2, 2, width, micro * length), BF),
        vm((micro, length, width), BF),
        vm((micro, length, width), BF),
        vm((2, PARTS, micro, length, half), BF),
        vm((PARTS, micro, length, half), BF),
        vm((PARTS, nx, nz * rows, half), BF),
        vm((PARTS, 2, nz * rows, half), BF),
        vm((PARTS, nz * rows, half), BF),
        vm((PARTS, nz * rows, half), BF),
        vm((nz, PARTS, rows, half), BF),
        vm((nz, PARTS, rows, half), BF),
        vm((2, PARTS, rows, half), BF),
        vm((micro, length, length), BF),
        vm((micro, length, width), BF),
        vm((nx, lx, wide), BF),
        vm((nx, lx, wide), BF),
        vm((nz, lz, wide), BF),
        vm((2, nz, lz, wide), BF),
        vm((micro, nx, lx, width), BF),
        vm((micro, nx, lx, width), BF),
        vm((micro, nz, lz, width), BF),
        vm((2, micro, nz, lz, width), BF),
        vm((own_rows, 2 * micro * length), BF),
        dma((9,)), dma((3 + 2 * micro,)), dma((micro, 2)), dma((micro, 2)), dma((1,)), dma((1,)),
        dma((PARTS, micro)), dma((PARTS, micro)),
        dma((PARTS,)), dma((PARTS,)), dma((PARTS,)), dma((PARTS,)),
        dma((nz, PARTS)), dma((nz, PARTS)), dma((1,)), dma((1,)),
        dma((micro, 2, 4)), dma((micro, 2)),
        dma((streams, nx)), dma((streams, nx)),
        dma((streams, nz)), dma((streams, nz)),
        dma((streams,)), dma((streams,)),
    ]
    return pl.pallas_call(
        functools.partial(kernel, dims),
        out_shape=(
            jax.ShapeDtypeStruct((own_rows, 2 * micro * length), BF),
            jax.ShapeDtypeStruct((2, micro, nz, lz, width), BF),
            jax.ShapeDtypeStruct((own_rows // LANES, LANES), F32),
            jax.ShapeDtypeStruct((2, PARTS, rows, half), BF),
        ),
        in_specs=[pl.BlockSpec(memory_space=pltpu.HBM)] * 6,
        out_specs=[pl.BlockSpec(memory_space=pltpu.HBM)] * 4,
        scratch_shapes=scratch,
        compiler_params=pltpu.CompilerParams(
            collective_id=0, has_side_effects=True, vmem_limit_bytes=56 << 20
        ),
    )(x, og, w_in, w_out, owner, slot)


def local(nz, nx, saved_input, out_grad, w_in, w_out, item_owner, item_slot, table, moment, second):
    ns = lax.axis_size("section")
    micro, length, width = out_grad.shape[0], out_grad.shape[2], out_grad.shape[3]
    owners = ns * nz * nx
    cap = max(2, 2 * BLOCK // owners)
    own_rows = table.shape[0]
    rows = width // (nz * nx)
    hot, tokens_in, hits, grads = exchange(
        (ns, nz, nx, cap),
        saved_input[0, :, 0],
        out_grad[:, 0],
        w_in[0],
        w_out[0],
        item_owner.reshape(micro, length),
        item_slot.reshape(micro, length),
        own_rows,
    )
    tokens = micro * length * nz * nx * lax.axis_size("replica")
    lines = (own_rows // LANES, LANES)
    shapes = [(rows, 4 * width), (rows, width), (own_rows, width), (own_rows, width), lines]
    grad_in, grad_out, table_new, moment_new, second_new = pl.pallas_call(
        functools.partial(finish, float(tokens) ** (-0.5)),
        out_shape=[jax.ShapeDtypeStruct(shape, F32) for shape in shapes],
        in_specs=[pl.BlockSpec(memory_space=pltpu.HBM)] * 7,
        out_specs=[pl.BlockSpec(memory_space=pltpu.HBM)] * 5,
        scratch_shapes=[pltpu.VMEM(part.shape, part.dtype) for part in (hot, tokens_in, hits, grads)]
        + [pltpu.VMEM(shape, F32) for shape in shapes[2:]]
        + [pltpu.VMEM(shape, F32) for shape in shapes]
        + [pltpu.SemaphoreType.DMA((4 + 3 * lines[0],)), pltpu.SemaphoreType.DMA((2 * lines[0] + 3,))],
        compiler_params=pltpu.CompilerParams(vmem_limit_bytes=56 << 20),
    )(hot, tokens_in, hits, grads, table, moment, second.reshape(lines))
    return (grad_in[None], grad_out[None], table_new, moment_new, second_new.reshape(own_rows))


def solution(mesh):
    nx = 4
    nz = mesh.shape["sample"] // nx
    placed = (
        P("section", None, ("sample", "replica"), None, None),
        P(None, ("sample", "replica"), None, None),
        P("section", None, None),
        P("section", None, None),
        P(("sample", "replica"), None, None, None),
        P(("sample", "replica"), None, None),
        P(("section", "sample"), None),
        P(("section", "sample"), None),
        P(("section", "sample")),
    )
    return jax.shard_map(
        functools.partial(local, nz, nx),
        mesh=mesh,
        in_specs=placed,
        out_specs=(
            P("section", "sample", None),
            P("section", "sample", None),
            P(("section", "sample"), None),
            P(("section", "sample"), None),
            P(("section", "sample")),
        ),
        check_vma=False,
    )
```

```python
import functools

import jax
import jax.numpy as jnp
from jax import lax
from jax.experimental import pallas as pl
from jax.experimental.pallas import tpu as pltpu
from jax.sharding import PartitionSpec as P

HEADS = 4
BLOCK = 64
LN_EPS = 1e-05
BETA_ONE = 0.8
BETA_TWO = 0.9
STEP_SIZE = 0.05
ADAM_EPS = 1e-08

F32 = jnp.float32
BF = jnp.bfloat16
MESH = pl.DeviceIdType.MESH
PARTS = 5
LANES = 128
LAG = 3


def mm(a, b):
    return jnp.dot(a, b, preferred_element_type=F32)


def mm_nt(a, b):
    return lax.dot_general(a, b, (((1,), (1,)), ((), ())), preferred_element_type=F32)


def sigmoid(v):
    return 0.5 + 0.5 * jnp.tanh(0.5 * v)


def mean(v):
    return jnp.mean(v, -1, keepdims=True)


def normed(v):
    center = v - mean(v)
    inverse = lax.rsqrt(mean(center * center) + LN_EPS)
    return center * inverse, inverse


def norm_back(grad, norm, inverse):
    return inverse * (grad - mean(grad) - norm * mean(grad * norm))


def slope(v, s):
    return s * (1.0 + v * (1.0 - s))


def kernel(
    dims,
    x_hbm, og_hbm, win_hbm, wout_hbm, owner_hbm, slot_hbm,
    oh_hbm, tt_hbm, hits_hbm, f_hbm,
    hits_ref, x_ref, win_ref, wout_ref, owner_ref, slot_ref,
    wint_s, woutt_s, vt_s, xn_s, rx_s, act_s, slope_s, w_s, zs_s, mn_s, rm_s,
    hx_s, hx_o, lt_s, g_s, below_s, d_s, d_r,
    gw_s, g1_r, g2_s, g2_r, gz_s, gz_r, f_s,
    p_s, tk_s, idp_s, idx_r, idz_s, idt_s, tp_s, tx_r, tz_s, tt_s, oh_s,
    in_ss, out_ss, hop_ss, hop_rs, hx_ss, hx_rs, d_ss, d_rs,
    g1_ss, g1_rs, g2_ss, g2_rs, gz_ss, gz_rs, f_ss, f_rs,
    tk_ss, tk_rs, ix_ss, ix_rs, iz_ss, iz_rs, ic_ss, ic_rs,
):
    ns, nz, nx, cap = dims
    micro, length, width = x_ref.shape
    half = width // 2
    mid = length // 2
    hs = width // HEADS
    scale = hs ** (-0.5)
    rows = width // (nz * nx)
    own_rows = oh_hbm.shape[0]
    piece = length // (nz * nx)
    sec = lax.axis_index("section")
    smp = lax.axis_index("sample")
    core = lax.axis_index("replica")
    zz, xx = lax.div(smp, nx), lax.rem(smp, nx)

    def wrap(v, n):
        return lax.rem(v, n)

    def x_peer(d):
        return (sec, zz * nx + wrap(xx + d, nx), core)

    z_order = sorted(range(1, nz), key=lambda d: -min(d, nz - d))

    def z_peer(d):
        return (sec, wrap(zz + d, nz) * nx + xx, core)

    other = (sec, smp, 1 - core)

    def remote(src, dst, ss, rs, dev):
        return pltpu.make_async_remote_copy(
            src_ref=src, dst_ref=dst, send_sem=ss, recv_sem=rs, device_id=dev, device_id_type=MESH
        )

    def load(i, src, dst):
        return pltpu.make_async_copy(src, dst, in_ss.at[i])

    def save(i, src, dst):
        return pltpu.make_async_copy(src, dst, out_ss.at[i])

    def save_tokens(c, m):
        return save(3 + 2 * m + jnp.where(c == core, 0, 1), tt_s.at[c, m], tt_hbm.at[c, m])

    loads = [load(0, x_hbm, x_ref)]
    for k in range(4):
        cols = pl.ds(k * width, width)
        loads.append(load(1 + k, win_hbm.at[:, cols], win_ref.at[:, cols]))
    loads.append(load(5, wout_hbm, wout_ref))
    loads.append(load(6, owner_hbm, owner_ref))
    loads.append(load(7, slot_hbm, slot_ref))
    for one in loads:
        one.start()

    @pl.when(sec == ns - 1)
    def _():
        load(8, og_hbm, g_s).start()

    barrier = pltpu.get_barrier_semaphore()
    peers = [other]
    peers += [(wrap(sec + d, ns), smp, core) for d in range(1, ns)]
    peers += [x_peer(d) for d in range(1, nx)]
    peers += [z_peer(d) for d in range(1, nz)]
    for peer in peers:
        pl.semaphore_signal(barrier, inc=1, device_id=peer, device_id_type=MESH)

    row_id = lax.broadcasted_iota(jnp.int32, (length, length), 0)
    col_id = lax.broadcasted_iota(jnp.int32, (length, length), 1)

    def forward():
        all_rows = micro * length
        loads[0].wait()
        xn, rx = normed(x_ref[...].reshape(all_rows, width).astype(F32))
        xn_s[...] = xn.reshape(xn_s.shape)
        rx_s[...] = rx.reshape(rx_s.shape)
        xb = xn.astype(BF)
        hx_s[1] = xb.reshape(micro, length, width)
        for k in range(4):
            loads[1 + k].wait()
            block = win_ref[:, k * width:(k + 1) * width]
            pre = mm(xb, block)
            s = sigmoid(pre)
            act = (pre * s).astype(BF)
            down = slope(pre, s)
            for m in range(micro):
                act_s[m, k] = act[m * length:(m + 1) * length]
                slope_s[m, k] = down[m * length:(m + 1) * length]
            wint_s[k] = block.T
        causal = row_id >= col_id
        for m in range(micro):
            vt_s[m] = act_s[m, 1].T
            mixed = []
            for h in range(HEADS):
                cols = slice(h * hs, (h + 1) * hs)
                z = mm_nt(act_s[m, 2, :, cols], act_s[m, 3, :, cols]) * scale
                s = sigmoid(z)
                wt = jnp.where(causal, z * s, 0.0).astype(BF)
                for r in range(2):
                    w_s[m, h, r] = wt[r * mid:(r + 1) * mid].T
                zs_s[m, h] = jnp.where(causal, slope(z, s), 0.0) * scale
                mixed.append(mm(wt, act_s[m, 1, :, cols]))
            mn, rm = normed(jnp.concatenate(mixed, -1))
            mn_s[m] = mn
            rm_s[m] = rm
            hx_s[0, m] = (mn * act_s[m, 0].astype(F32)).astype(BF)
        loads[5].wait()
        woutt_s[...] = wout_ref[...].T

    first = jnp.where(core == 0, 1, nx - 1)
    second = nx - first

    def flip(v, mask):
        pair = v + 1 - 2 * lax.rem(v, 2)
        return jnp.where(mask == 1, pair, nx - 1 - v)

    def x_at(x):
        return (sec, zz * nx + x, core)

    def g1_copy(k):
        return remote(
            gw_s.at[k, pl.ds(2, 2)], g1_r.at[k], g1_ss.at[k], g1_rs.at[k], x_at(flip(xx, first))
        )

    def g2_copy(k):
        return remote(g2_s.at[k], g2_r.at[k], g2_ss.at[k], g2_rs.at[k], x_at(flip(xx, second)))

    def gz_copy(k, d):
        return remote(
            gz_s.at[wrap(zz + d, nz), k], gz_r.at[d, k], gz_ss.at[d, k], gz_rs.at[d, k], z_peer(d)
        )

    def d_copy(k, m):
        return remote(d_s.at[1 - core, k, m], d_r.at[k, m], d_ss.at[k, m], d_rs.at[k, m], other)

    def gradient(k, kind):
        for m in range(micro):
            d_copy(k, m).wait_recv()
        part = mm(lt_s[kind, 0], d_s[core, k].reshape(micro * length, half))
        part = part + mm(lt_s[kind, 1], d_r[k].reshape(micro * length, half))
        part = part.astype(BF)
        for x in range(nx):
            slot = jnp.where(
                xx == x, 0, jnp.where(flip(xx, second) == x, 1, jnp.where(flip(xx, first) == x, 2, 3))
            )
            for z in range(nz):
                at = (z * nx + x) * rows
                gw_s[k, slot, z * rows:(z + 1) * rows, :] = part[at:at + rows]
        g1_copy(k).start()

    def keep(m, k, at, value):
        d_s[0, k, m, at] = value[:, :half]
        d_s[1, k, m, at] = value[:, half:]

    def backward(m, r, carried):
        at = slice(r * mid, (r + 1) * mid)
        g = g_s[m, at]
        keep(m, 0, at, g)
        if r == 0:
            d_copy(0, m).start()
        dh = mm(g, woutt_s[...])
        mn = mn_s[m, at]
        dpre = [(dh * mn * slope_s[m, 0, at]).astype(BF)]
        dmix = norm_back(dh * act_s[m, 0, at].astype(F32), mn, rm_s[m, at]).astype(BF)
        dv, dq, dk = [], [], []
        for h in range(HEADS):
            cols = slice(h * hs, (h + 1) * hs)
            dm = dmix[:, cols]
            dw = mm(dm, vt_s[m, cols])
            dv.append(mm(w_s[m, h, r], dm))
            dz = (dw * zs_s[m, h, at]).astype(BF)
            dq.append(mm(dz, act_s[m, 3, :, cols]))
            dk.append(mm(dz.T, act_s[m, 2, at, cols]))
        dv, dq, dk = (jnp.concatenate(part, -1) for part in (dv, dq, dk))
        if r == 1:
            carried = (dv[:mid], dk[:mid])
            dv, dk = dv[mid:], dk[mid:]
        else:
            dv, dk = dv[:mid] + carried[0], dk[:mid] + carried[1]
        for k, part in enumerate((dv, dq, dk)):
            dpre.append((part * slope_s[m, k + 1, at]).astype(BF))
        for k in range(4):
            keep(m, k + 1, at, dpre[k])
            if r == 0:
                d_copy(k + 1, m).start()
        dxn = mm(dpre[0], wint_s[0])
        for k in range(1, 4):
            dxn = dxn + mm(dpre[k], wint_s[k])
        below = norm_back(dxn, xn_s[m, at], rx_s[m, at]) + g.astype(F32)
        below_s[m, at] = below.astype(BF)
        return carried

    def pack_plan(m):
        owner = owner_ref[m:m + 1, :]
        spread = jnp.broadcast_to(owner.astype(F32), (length, length))
        same = (spread == spread.T) & (lax.div(row_id, BLOCK) == lax.div(col_id, BLOCK)) & (row_id < col_id)
        rank = jnp.sum(jnp.where(same, 1.0, 0.0), 0, keepdims=True).astype(jnp.int32)
        place = owner - sec * (nz * nx)
        mine = (place >= 0) & (place < nz * nx)
        place = jnp.where(mine, place, 0)
        block = lax.div(lax.broadcasted_iota(jnp.int32, (1, length), 1), BLOCK)
        to = (lax.rem(place, nx) * nz + lax.div(place, nx)) * piece + block * cap + rank
        to = jnp.where(mine, to, -1)
        plan = jnp.where(row_id == to, 1.0, 0.0).astype(BF)
        p_s[m] = plan
        name = slot_ref[m:m + 1, :] + 1
        high, low = lax.div(name, 32), lax.rem(name, 32)
        both = jnp.where(row_id < length // 2, high, low).astype(F32).astype(BF)
        return mm_nt(plan, both).astype(BF)

    def x_start(pack, inbox, ss, rs):
        inbox[0] = pack[xx]
        for d in range(1, nx):
            remote(pack.at[wrap(xx + d, nx)], inbox.at[d], ss.at[d], rs.at[d], x_peer(d)).start()

    def z_start(inbox, outbox, total, xs, xr, ss, rs):
        for d in range(1, nx):
            remote(inbox.at[d], inbox.at[d], xs.at[d], xr.at[d], x_peer(d)).wait_recv()
        src = lax.div(lax.rem(row_id, nx * piece), piece) * (nz * piece)
        src = src + lax.div(row_id, nx * piece) * piece + lax.rem(row_id, piece)
        turn = jnp.where(src == col_id, 1.0, 0.0).astype(BF)
        stacked = inbox[...].reshape(length, inbox.shape[-1])
        moved = mm(turn, stacked).astype(BF)
        outbox[...] = moved.reshape(outbox.shape)
        total[0] = outbox[zz]
        for d in z_order:
            remote(outbox.at[wrap(zz + d, nz)], total.at[d], ss.at[d], rs.at[d], z_peer(d)).start()

    def core_start(mine, zs, zr, ss, rs):
        for d in range(1, nz):
            remote(mine.at[d], mine.at[d], zs.at[d], zr.at[d], z_peer(d)).wait_recv()
        remote(mine, mine, ss, rs, other).start()

    def prepare_own():
        ids = jnp.concatenate([pack_plan(m) for m in range(micro)], -1)
        idp_s[...] = ids.reshape(idp_s.shape)
        for kind in range(2):
            lt_s[kind, 0] = hx_s[kind].reshape(micro * length, width).T

    def prepare_sends():
        remote(hx_s, hx_o, hx_ss.at[0], hx_rs.at[0], other).start()
        x_start(idp_s, idx_r, ix_ss.at[0], ix_rs.at[0])

    def ids_along_z():
        z_start(idx_r, idz_s, idt_s.at[core], ix_ss.at[0], ix_rs.at[0], iz_ss.at[0], iz_rs.at[0])

    def prepare_other():
        remote(hx_s, hx_o, hx_ss.at[0], hx_rs.at[0], other).wait_recv()
        for kind in range(2):
            lt_s[kind, 1] = hx_o[kind].reshape(micro * length, width).T

    def ids_over():
        core_start(idt_s.at[core], iz_ss.at[0], iz_rs.at[0], ic_ss.at[0], ic_rs.at[0])

    def ids_done():
        remote(idt_s.at[1 - core], idt_s.at[1 - core], ic_ss.at[0], ic_rs.at[0], other).wait_recv()
        hits = jnp.zeros((own_rows, 1), F32)
        own_id = lax.broadcasted_iota(jnp.int32, (own_rows, length), 0).astype(F32)
        for c in range(2):
            for m in range(micro):
                both = idt_s[c, :, :, m * LANES:(m + 1) * LANES].reshape(length, LANES).astype(F32).T
                name = both[:1] * 32.0 + both[LANES // 2:LANES // 2 + 1] - 1.0
                hot = jnp.where(own_id == name, 1.0, 0.0)
                hits = hits + jnp.sum(hot, -1, keepdims=True)
                oh_s[:, (c * micro + m) * length:(c * micro + m + 1) * length] = hot.astype(BF)
        for b in range(own_rows // LANES):
            column = hits[b * LANES:(b + 1) * LANES]
            hits_ref[b:b + 1, :] = jnp.broadcast_to(column, (LANES, LANES)).T[:1]
        save(0, hits_ref, hits_hbm).start()
        save(2, oh_s, oh_hbm).start()

    forward()
    for one in loads[6:]:
        one.wait()

    @pl.when(sec == ns - 1)
    def _():
        load(8, og_hbm, g_s).wait()

    pl.semaphore_wait(barrier, len(peers))

    early = ns // 2

    @pl.when(sec < ns - 1)
    def _():
        prepare_own()
        prepare_sends()

    @pl.when(sec < early)
    def _():
        ids_along_z()
        prepare_other()
        ids_over()
        ids_done()

    def hop(m, r):
        at = pl.ds(r * mid, mid)
        return remote(
            below_s.at[m, at], g_s.at[m, at], hop_ss.at[m, r], hop_rs.at[m, r],
            (wrap(sec + ns - 1, ns), smp, core),
        )

    def token(m, r, to):
        at = pl.ds(r * mid, mid)
        return remote(
            below_s.at[m, at], tk_s.at[m, at], tk_ss.at[m, r, to], tk_rs.at[m, r], (to, smp, core)
        )

    far_first = sorted(range(1, ns), key=lambda to: -min(to, ns - to))

    def pack(m):
        packed = mm(p_s[m], tk_s[m]).astype(BF)
        tp_s[m] = packed.reshape(tp_s.shape[1:])
        x_start(tp_s.at[m], tx_r.at[m], ix_ss.at[1 + m], ix_rs.at[1 + m])

    @pl.loop(0, micro)
    def _(m):
        carried = None
        for r in (1, 0):
            @pl.when(sec < ns - 1)
            def _():
                hop(m, r).wait_recv()

            carried = backward(m, r, carried)

            @pl.when(sec > 0)
            def _():
                hop(m, r).start()

            @pl.when(sec == 0)
            def _():
                for to in far_first:
                    token(m, r, to).start()

        @pl.when(sec == 0)
        def _():
            tk_s[m] = below_s[m]

            @pl.when(m < micro - 1)
            def _():
                pack(m)

    @pl.when(sec == ns - 1)
    def _():
        prepare_own()
        prepare_sends()

    @pl.when(sec >= early)
    def _():
        prepare_other()

    def get_tokens(m):
        @pl.when(sec > 0)
        def _():
            for r in range(2):
                token(m, r, 1).wait_recv()

        pack(m)

    def by_section(places):
        at = jnp.int32(places[-1])
        for number in range(len(places) - 2, -1, -1):
            at = jnp.where(sec == number, places[number], at)
        return at

    def on_step(step, places, action):
        start = [by_section(place) for place in places]

        @pl.when((step == start[0]) | (step == start[1]))
        def _():
            action(jnp.where(step == start[1], 1, 0))

    def send_over(m):
        core_start(tt_s.at[core, m], iz_ss.at[1 + m], iz_rs.at[1 + m], ic_ss.at[1 + m], ic_rs.at[1 + m])
        save_tokens(core, m).start()

    @pl.loop(0, 10)
    def _(step):
        @pl.when(step < PARTS)
        def _():
            gradient(step, jnp.minimum(step, 1))

        @pl.when((step >= LAG) & (step < PARTS + LAG))
        def _():
            k = step - LAG
            g1_copy(k).wait_recv()
            total = gw_s[k, 1].astype(F32) + g1_r[k, 1].astype(F32)
            g2_s[k] = total.astype(BF)
            g2_copy(k).start()

        @pl.when((step > LAG) & (step <= PARTS + LAG))
        def _():
            k = step - LAG - 1
            g2_copy(k).wait_recv()
            total = gw_s[k, 0].astype(F32) + g1_r[k, 0].astype(F32) + g2_r[k].astype(F32)
            total = total.astype(BF)
            for z in range(nz):
                gz_s[z, k] = total[z * rows:(z + 1) * rows]
            for d in z_order:
                gz_copy(k, d).start()

        for place, action in ((1, ids_along_z), (3, ids_over), (5, ids_done)):
            @pl.when((step == place) & (sec >= early))
            def _():
                action()

        on_step(step, ((-1, 4, 5, 6), (1, 5, 6, 7)), get_tokens)
        on_step(
            step, ((2, 5, 6, 7), (4, 7, 7, 8)),
            lambda m: z_start(
                tx_r.at[m], tz_s.at[m], tt_s.at[core, m],
                ix_ss.at[1 + m], ix_rs.at[1 + m], iz_ss.at[1 + m], iz_rs.at[1 + m],
            ),
        )
        on_step(
            step, ((6, 7, 8, 8), (8, 8, 9, 9)),
            send_over,
        )

    total = gz_s[zz].astype(F32)
    for d in range(1, nz):
        for k in range(PARTS):
            gz_copy(k, d).wait_recv()
        total = total + gz_r[d].astype(F32)
    f_s[core] = total.astype(BF)
    remote(f_s.at[core], f_s.at[core], f_ss.at[0], f_rs.at[0], other).start()

    for m in range(micro):
        remote(
            tt_s.at[1 - core, m], tt_s.at[1 - core, m], ic_ss.at[1 + m], ic_rs.at[1 + m], other
        ).wait_recv()
        save_tokens(1 - core, m).start()
    remote(f_s.at[1 - core], f_s.at[1 - core], f_ss.at[0], f_rs.at[0], other).wait_recv()
    save(1, f_s, f_hbm).start()

    remote(hx_s, hx_o, hx_ss.at[0], hx_rs.at[0], other).wait_send()
    remote(f_s.at[core], f_s.at[core], f_ss.at[0], f_rs.at[0], other).wait_send()

    @pl.loop(0, PARTS)
    def _(k):
        for m in range(micro):
            d_copy(k, m).wait_send()
        g1_copy(k).wait_send()
        g2_copy(k).wait_send()
        for d in range(1, nz):
            gz_copy(k, d).wait_send()

    for i in range(1 + micro):
        pack_from = idp_s if i == 0 else tp_s.at[i - 1]
        inbox = idx_r if i == 0 else tx_r.at[i - 1]
        outbox = idz_s if i == 0 else tz_s.at[i - 1]
        full = idt_s.at[core] if i == 0 else tt_s.at[core, i - 1]
        for d in range(1, nx):
            remote(
                pack_from.at[wrap(xx + d, nx)], inbox.at[d], ix_ss.at[i, d], ix_rs.at[i, d], x_peer(d)
            ).wait_send()
        for d in range(1, nz):
            remote(
                outbox.at[wrap(zz + d, nz)], full.at[d], iz_ss.at[i, d], iz_rs.at[i, d], z_peer(d)
            ).wait_send()
        remote(full, full, ic_ss.at[i], ic_rs.at[i], other).wait_send()
    @pl.when(sec > 0)
    def _():
        for m in range(micro):
            for r in range(2):
                hop(m, r).wait_send()

    for m in range(micro):
        @pl.when(sec == 0)
        def _():
            for to in range(1, ns):
                for r in range(2):
                    token(m, r, to).wait_send()

    save(0, hits_ref, hits_hbm).wait()
    save(1, f_s, f_hbm).wait()
    save(2, oh_s, oh_hbm).wait()
    for m in range(micro):
        for c in (core, 1 - core):
            save_tokens(c, m).wait()


def finish(
    factor,
    oh_hbm, tt_hbm, hits_hbm, f_hbm, table_in, moment_in, second_in,
    gi_hbm, go_hbm, table_hbm, moment_hbm, second_hbm,
    oh_ref, tt_ref, hits_ref, f_ref, table_ref, moment_ref, second_ref, gi_s, go_s, table_s, moment_s, second_s, in_sems, sems,
):
    half = f_ref.shape[-1]
    width = 2 * half
    blocks = oh_ref.shape[0] // LANES

    copies = []

    loads = [
        pltpu.make_async_copy(src, dst, in_sems.at[i])
        for i, (src, dst) in enumerate(((tt_hbm, tt_ref), (hits_hbm, hits_ref), (second_in, second_ref), (f_hbm, f_ref)))
    ]

    def row_loads(b):
        at = pl.ds(b * LANES, LANES)
        pairs = ((oh_hbm, oh_ref), (moment_in, moment_ref), (table_in, table_ref))
        return [
            pltpu.make_async_copy(src.at[at], dst.at[at], in_sems.at[4 + 3 * b + i])
            for i, (src, dst) in enumerate(pairs)
        ]

    for load in loads[:3]:
        load.start()
    for b in range(blocks):
        for load in row_loads(b):
            load.start()
    loads[3].start()
    for load in loads[:3]:
        load.wait()
    tokens = tt_ref[...].reshape(oh_ref.shape[1], width)

    def put(src, dst):
        copy = pltpu.make_async_copy(src, dst, sems.at[len(copies)])
        copy.start()
        copies.append(copy)

    for b in range(blocks):
        at = pl.ds(b * LANES, LANES)
        for load in row_loads(b):
            load.wait()
        grad = mm(oh_ref[at, :], tokens)
        hit = jnp.broadcast_to(hits_ref[b:b + 1, :], (LANES, LANES)).T > 0.5
        wide = jnp.concatenate([hit] * (width // LANES), -1)
        square = jnp.mean(grad * grad, -1, keepdims=True)
        square = jnp.broadcast_to(square, (LANES, LANES))
        old = jnp.broadcast_to(second_ref[b:b + 1, :], (LANES, LANES)).T
        new = jnp.where(hit, BETA_TWO * old + (1.0 - BETA_TWO) * square, old)
        second_s[b:b + 1, :] = new.T[:1]
        old_moment = moment_ref[at, :]
        moment = jnp.where(wide, BETA_ONE * old_moment + (1.0 - BETA_ONE) * grad, old_moment)
        moment_s[at, :] = moment
        put(moment_s.at[at], moment_hbm.at[at])
        old_table = table_ref[at, :]
        below = jnp.concatenate([jnp.sqrt(new) + ADAM_EPS] * (width // LANES), -1)
        table_s[at, :] = jnp.where(wide, old_table - STEP_SIZE * moment / below, old_table)
        put(table_s.at[at], table_hbm.at[at])
    put(second_s, second_hbm)
    loads[3].wait()
    for c in range(2):
        go_s[:, c * half:(c + 1) * half] = f_ref[c, 0].astype(F32) * factor
        for k in range(4):
            at = k * width + c * half
            gi_s[:, at:at + half] = f_ref[c, k + 1].astype(F32) * factor
    put(go_s, go_hbm)
    put(gi_s, gi_hbm)
    for copy in copies:
        copy.wait()


def exchange(dims, x, og, w_in, w_out, owner, slot, own_rows):
    ns, nz, nx, cap = dims
    micro, length, width = x.shape
    half = width // 2
    rows = width // (nz * nx)
    dma = pltpu.SemaphoreType.DMA
    vm = pltpu.VMEM
    lx, lz = length // nx, length // nz
    streams = 1 + micro
    wide = LANES * micro
    scratch = [
        vm((own_rows // LANES, LANES), F32),
        vm((micro, length, width), BF),
        vm((width, 4 * width), BF),
        vm((width, width), BF),
        vm((micro, length), jnp.int32),
        vm((micro, length), jnp.int32),
        vm((4, width, width), BF),
        vm((width, width), BF),
        vm((micro, width, length), BF),
        vm((micro, length, width), F32),
        vm((micro, length, 1), F32),
        vm((micro, 4, length, width), BF),
        vm((micro, 4, length, width), F32),
        vm((micro, HEADS, 2, length, length // 2), BF),
        vm((micro, HEADS, length, length), F32),
        vm((micro, length, width), F32),
        vm((micro, length, 1), F32),
        vm((2, micro, length, width), BF),
        vm((2, micro, length, width), BF),
        vm((2, 2, width, micro * length), BF),
        vm((micro, length, width), BF),
        vm((micro, length, width), BF),
        vm((2, PARTS, micro, length, half), BF),
        vm((PARTS, micro, length, half), BF),
        vm((PARTS, nx, nz * rows, half), BF),
        vm((PARTS, 2, nz * rows, half), BF),
        vm((PARTS, nz * rows, half), BF),
        vm((PARTS, nz * rows, half), BF),
        vm((nz, PARTS, rows, half), BF),
        vm((nz, PARTS, rows, half), BF),
        vm((2, PARTS, rows, half), BF),
        vm((micro, length, length), BF),
        vm((micro, length, width), BF),
        vm((nx, lx, wide), BF),
        vm((nx, lx, wide), BF),
        vm((nz, lz, wide), BF),
        vm((2, nz, lz, wide), BF),
        vm((micro, nx, lx, width), BF),
        vm((micro, nx, lx, width), BF),
        vm((micro, nz, lz, width), BF),
        vm((2, micro, nz, lz, width), BF),
        vm((own_rows, 2 * micro * length), BF),
        dma((9,)), dma((3 + 2 * micro,)), dma((micro, 2)), dma((micro, 2)), dma((1,)), dma((1,)),
        dma((PARTS, micro)), dma((PARTS, micro)),
        dma((PARTS,)), dma((PARTS,)), dma((PARTS,)), dma((PARTS,)),
        dma((nz, PARTS)), dma((nz, PARTS)), dma((1,)), dma((1,)),
        dma((micro, 2, 4)), dma((micro, 2)),
        dma((streams, nx)), dma((streams, nx)),
        dma((streams, nz)), dma((streams, nz)),
        dma((streams,)), dma((streams,)),
    ]
    return pl.pallas_call(
        functools.partial(kernel, dims),
        out_shape=(
            jax.ShapeDtypeStruct((own_rows, 2 * micro * length), BF),
            jax.ShapeDtypeStruct((2, micro, nz, lz, width), BF),
            jax.ShapeDtypeStruct((own_rows // LANES, LANES), F32),
            jax.ShapeDtypeStruct((2, PARTS, rows, half), BF),
        ),
        in_specs=[pl.BlockSpec(memory_space=pltpu.HBM)] * 6,
        out_specs=[pl.BlockSpec(memory_space=pltpu.HBM)] * 4,
        scratch_shapes=scratch,
        compiler_params=pltpu.CompilerParams(
            collective_id=0, has_side_effects=True, vmem_limit_bytes=56 << 20
        ),
    )(x, og, w_in, w_out, owner, slot)


def local(nz, nx, saved_input, out_grad, w_in, w_out, item_owner, item_slot, table, moment, second):
    ns = lax.axis_size("section")
    micro, length, width = out_grad.shape[0], out_grad.shape[2], out_grad.shape[3]
    owners = ns * nz * nx
    cap = max(2, 2 * BLOCK // owners)
    own_rows = table.shape[0]
    rows = width // (nz * nx)
    hot, tokens_in, hits, grads = exchange(
        (ns, nz, nx, cap),
        saved_input[0, :, 0],
        out_grad[:, 0],
        w_in[0],
        w_out[0],
        item_owner.reshape(micro, length),
        item_slot.reshape(micro, length),
        own_rows,
    )
    tokens = micro * length * nz * nx * lax.axis_size("replica")
    lines = (own_rows // LANES, LANES)
    shapes = [(rows, 4 * width), (rows, width), (own_rows, width), (own_rows, width), lines]
    grad_in, grad_out, table_new, moment_new, second_new = pl.pallas_call(
        functools.partial(finish, float(tokens) ** (-0.5)),
        out_shape=[jax.ShapeDtypeStruct(shape, F32) for shape in shapes],
        in_specs=[pl.BlockSpec(memory_space=pltpu.HBM)] * 7,
        out_specs=[pl.BlockSpec(memory_space=pltpu.HBM)] * 5,
        scratch_shapes=[pltpu.VMEM(part.shape, part.dtype) for part in (hot, tokens_in, hits, grads)]
        + [pltpu.VMEM(shape, F32) for shape in shapes[2:]]
        + [pltpu.VMEM(shape, F32) for shape in shapes]
        + [pltpu.SemaphoreType.DMA((4 + 3 * lines[0],)), pltpu.SemaphoreType.DMA((2 * lines[0] + 3,))],
        compiler_params=pltpu.CompilerParams(vmem_limit_bytes=56 << 20),
    )(hot, tokens_in, hits, grads, table, moment, second.reshape(lines))
    return (grad_in[None], grad_out[None], table_new, moment_new, second_new.reshape(own_rows))


def solution(mesh):
    nx = 4
    nz = mesh.shape["sample"] // nx
    placed = (
        P("section", None, ("sample", "replica"), None, None),
        P(None, ("sample", "replica"), None, None),
        P("section", None, None),
        P("section", None, None),
        P(("sample", "replica"), None, None, None),
        P(("sample", "replica"), None, None),
        P(("section", "sample"), None),
        P(("section", "sample"), None),
        P(("section", "sample")),
    )
    return jax.shard_map(
        functools.partial(local, nz, nx),
        mesh=mesh,
        in_specs=placed,
        out_specs=(
            P("section", "sample", None),
            P("section", "sample", None),
            P(("section", "sample"), None),
            P(("section", "sample"), None),
            P(("section", "sample")),
        ),
        check_vma=False,
    )
```
